32 devices in a mesh: traj: 4 (over y, x), slab: 8 (over z, core).
Axes of the slice: x: 2, y: 2, z: 4, core: 2. Of those that a mesh axis runs over, the one named last changes fastest.
Arguments:
- grad_out: bfloat16 [64, 24, 128], P(('traj', 'slab')), parts along dimension 0, may hold values from -24 to 24
- cached: bfloat16 [64, 24, 128], P('traj', 'slab'), parts along dimension 0, may hold values from -0.059814453 to 0.059814453
- values: bfloat16 [64, 24, 128], P(('traj', 'slab')), parts along dimension 0, may hold values from -0.1796875 to 0.1796875
- query_x: bfloat16 [64, 128], P('traj'), parts along dimension 0, may hold values from -6 to 6
- key_x: bfloat16 [64, 128], P('traj'), parts along dimension 0, may hold values from -6 to 6
- query_y: bfloat16 [96, 128], P('traj'), parts along dimension 0, may hold values from -6 to 6
- key_y: bfloat16 [96, 128], P('traj'), parts along dimension 0, may hold values from -6 to 6
Outputs:
- grad_values: bfloat16 [64, 24, 128], P(('traj', 'slab')), parts along dimension 0
- query_x_grad: float32 [64, 128], P(('traj', 'slab')), parts along dimension 0
- key_x_grad: float32 [64, 128], P(('traj', 'slab')), parts along dimension 0
- query_y_grad: float32 [96, 128], P(('traj', 'slab')), parts along dimension 0
- key_y_grad: float32 [96, 128], P(('traj', 'slab')), parts along dimension 0
The draws below stay inside these ranges and needn't reach their ends.
There are 4 independent parts, one for each index of `traj`. The reference program is written for one: setup_inputs(seed, part) draws one part's arguments, and reference() takes and returns one part's arrays. A program takes and returns all parts, laid end to end along the dimension named above; each array names one. Nothing has to cross between parts.
All inputs are finite; a program needn't handle non-finite values.
Results may differ from the reference program's by a relative error of at most 0.0067.
Values may be sent and summed in bfloat16 or wider, within the bound.
A program may use at most 64 MiB of HBM per device.

```python
import math
import jax
import jax.numpy as jnp
from jax import lax

HEADS = 4
HEAD = 32
CHANNELS = 128
NX = 16
NY = 24


def factor_pair(key, length):
    pieces = jax.random.split(key, 2)
    queries = jnp.clip(1.4 * jax.random.normal(pieces[0], (length, CHANNELS), jnp.float32), -6.0, 6.0)
    key_rows = jnp.clip(1.4 * jax.random.normal(pieces[1], (length, CHANNELS), jnp.float32), -6.0, 6.0)
    return (queries, key_rows)


def draw_query_x(key, part):
    return factor_pair(jax.random.fold_in(key, 11), NX)[0].astype(jnp.bfloat16)


def draw_key_x(key, part):
    return factor_pair(jax.random.fold_in(key, 11), NX)[1].astype(jnp.bfloat16)


def draw_query_y(key, part):
    return factor_pair(jax.random.fold_in(key, 12), NY)[0].astype(jnp.bfloat16)


def draw_key_y(key, part):
    return factor_pair(jax.random.fold_in(key, 12), NY)[1].astype(jnp.bfloat16)


def with_spikes(array, rng, source, target, shards_of, factor):
    def block_of(dim):
        return (jnp.arange(array.shape[dim]) // (array.shape[dim] // shards_of)).reshape((-1,) + (1,) * (array.ndim - 1 - dim))

    first = jax.random.permutation(rng, shards_of)[block_of(target)]
    far = (block_of(target) + shards_of // 2) % shards_of
    return jnp.where((block_of(source) == first) | (block_of(source) == far), factor * array, array)


def levels(stream_key, shape, shards, low, high):
    level = 1.0
    for dim, shards_of in shards:
        heights = jax.random.uniform(jax.random.fold_in(jax.random.fold_in(stream_key, 6), dim), (shards_of,), jnp.float32, low / len(shards), high / len(shards))
        level = level * jnp.repeat(jnp.exp(heights), shape[dim] // shards_of).reshape((-1,) + (1,) * (len(shape) - 1 - dim))
    return level


def noise(stream_key, shape, spread, reach, shards=(), dtype=jnp.bfloat16):
    array = spread * jax.random.normal(stream_key, shape, jnp.float32)
    if shards:
        array = array * levels(stream_key, shape, shards, -0.22, 0.18)
    return jnp.clip(array, -reach, reach).astype(dtype)


def heavy_noise(stream_key, dims, spread, most, shards, heavy, dtype=jnp.bfloat16):
    values = spread * jax.random.normal(stream_key, dims, jnp.float32)
    if shards:
        values = values * levels(stream_key, dims, shards, -0.22, 0.18)
    return jnp.clip(with_spikes(values, jax.random.fold_in(stream_key, 3), *heavy), -most, most).astype(dtype)


def setup_inputs(seed: int = 0, part: int = 0) -> dict:
    arg_keys = jax.random.split(jax.random.key(seed), 8)
    part_keys = jax.random.split(jax.random.fold_in(arg_keys[7], part), 8)
    return {
        "grad_out": heavy_noise(part_keys[0], (NX, NY, CHANNELS), 4.0, 24.0, ((0, 8),), (1, 0, 8, 2.0)),
        "cached": noise(part_keys[1], (NX, NY, CHANNELS), 0.01, 0.059814453, ((1, 8),)),
        "values": heavy_noise(part_keys[2], (NX, NY, CHANNELS), 0.03, 0.1796875, ((0, 8),), (0, 1, 8, 2.0)),
        "query_x": draw_query_x(jax.random.fold_in(jax.random.fold_in(arg_keys[7], part), 71), part),
        "key_x": draw_key_x(jax.random.fold_in(jax.random.fold_in(arg_keys[7], part), 71), part),
        "query_y": draw_query_y(jax.random.fold_in(jax.random.fold_in(arg_keys[7], part), 71), part),
        "key_y": draw_key_y(jax.random.fold_in(jax.random.fold_in(arg_keys[7], part), 71), part),
    }


def axis_kernel(queries, key_rows):
    scores = jnp.dot(queries, key_rows.T, preferred_element_type=jnp.float32) / math.sqrt(HEAD)
    return jax.nn.softmax(scores, axis=1)

def factor_grads(kernel, coupling, queries, key_rows):
    row_delta = lax.optimization_barrier(jnp.sum(kernel * coupling, axis=1))
    weighted = kernel * (coupling - row_delta[:, None])
    grad_query = jnp.dot(weighted, key_rows.astype(jnp.float32), precision=lax.Precision.HIGHEST) / math.sqrt(HEAD)
    grad_key = jnp.dot(weighted.T, queries.astype(jnp.float32), precision=lax.Precision.HIGHEST) / math.sqrt(HEAD)
    return (grad_query, grad_key)

def reference(grad_out, cached, values, query_x, key_x, query_y, key_y):
    mixed_heads = []
    qx_terms = []
    kx_terms = []
    for head_index in range(HEADS):
        offset = head_index * HEAD
        head_query = query_x[:, offset:offset + HEAD]
        head_key = key_x[:, offset:offset + HEAD]
        kernel = axis_kernel(head_query, head_key)
        grad_rows = grad_out[:, :, offset:offset + HEAD].reshape(NX, NY * HEAD)
        saved_rows = cached[:, :, offset:offset + HEAD].reshape(NX, NY * HEAD)
        grad_mixed = lax.dot_general(kernel.astype(jnp.bfloat16), grad_rows, (((0,), (0,)), ((), ())), preferred_element_type=jnp.float32).astype(jnp.bfloat16)
        coupling = lax.dot_general(grad_rows, saved_rows, (((1,), (1,)), ((), ())), preferred_element_type=jnp.float32)
        grad_query, grad_key = factor_grads(kernel, coupling, head_query, head_key)
        qx_terms.append(grad_query)
        kx_terms.append(grad_key)
        mixed_heads.append(grad_mixed.reshape(NX, NY, HEAD))
    value_heads = []
    qy_terms = []
    ky_terms = []
    for head_index in range(HEADS):
        offset = head_index * HEAD
        head_query = query_y[:, offset:offset + HEAD]
        head_key = key_y[:, offset:offset + HEAD]
        kernel = axis_kernel(head_query, head_key)
        kernel_low = lax.optimization_barrier(kernel.astype(jnp.bfloat16)).astype(jnp.float32)
        mixed_head = mixed_heads[head_index].astype(jnp.float32)
        value_head = values[:, :, offset:offset + HEAD].astype(jnp.float32)
        grad_value = jnp.einsum('jk,xje->xke', kernel_low, mixed_head, precision=lax.Precision.HIGHEST)
        coupling = jnp.einsum('xje,xke->jk', mixed_head, value_head, precision=lax.Precision.HIGHEST)
        grad_query, grad_key = factor_grads(kernel, coupling, head_query, head_key)
        qy_terms.append(grad_query)
        ky_terms.append(grad_key)
        value_heads.append(grad_value.astype(jnp.bfloat16))
    return (jnp.concatenate(value_heads, axis=2), jnp.concatenate(qx_terms, axis=1), jnp.concatenate(kx_terms, axis=1), jnp.concatenate(qy_terms, axis=1), jnp.concatenate(ky_terms, axis=1))
```

```python
import functools
import math

import jax
import jax.numpy as jnp
from jax import lax
from jax.experimental import pallas as pl
from jax.experimental.pallas import tpu as pltpu
from jax.sharding import PartitionSpec as P

HEADS = 4
HEAD = 32
CHANNELS = HEADS * HEAD


def axis_kernel(queries, key_rows):
    scores = jnp.dot(queries, key_rows.T, preferred_element_type=jnp.float32) / math.sqrt(HEAD)
    return jax.nn.softmax(scores, axis=1)


def local_terms(kernel, coupling, queries, key_rows):
    row_delta = jnp.sum(kernel * coupling, axis=1)
    weighted = kernel * coupling
    grad_query = jnp.dot(
        weighted, key_rows.astype(jnp.float32), precision=lax.Precision.HIGHEST
    ) / math.sqrt(HEAD)
    grad_key = jnp.dot(
        weighted.T, queries.astype(jnp.float32), precision=lax.Precision.HIGHEST
    ) / math.sqrt(HEAD)
    return (grad_query, grad_key, row_delta)


def corrections(own_rows, own_cols, delta_total, queries, key_rows, start, count):
    own_delta = lax.dynamic_slice_in_dim(delta_total, start, count, 0)
    query_fix = (
        own_delta[:, None]
        * jnp.dot(own_rows, key_rows.astype(jnp.float32), precision=lax.Precision.HIGHEST)
        / math.sqrt(HEAD)
    )
    key_fix = jnp.dot(
        own_cols.T,
        delta_total[:, None] * queries.astype(jnp.float32),
        precision=lax.Precision.HIGHEST,
    ) / math.sqrt(HEAD)
    return (query_fix, key_fix)


def exchanged_form(grad_out, cached, values, query_x, key_x, query_y, key_y):
    index = lax.axis_index("slab")
    x_rows = grad_out.shape[0]
    x_count = cached.shape[0]
    y_rows = cached.shape[1]
    x_start = index * x_rows
    y_start = index * y_rows
    grad_columns = lax.all_to_all(grad_out, "slab", split_axis=1, concat_axis=0, tiled=True)
    mixed_heads = []
    query_terms = []
    key_terms = []
    delta_terms = []
    row_slices = []
    col_slices = []
    for head_index in range(HEADS):
        offset = head_index * HEAD
        head_query = query_x[:, offset : offset + HEAD]
        head_key = key_x[:, offset : offset + HEAD]
        kernel = axis_kernel(head_query, head_key)
        grad_rows = grad_columns[:, :, offset : offset + HEAD].reshape(x_count, y_rows * HEAD)
        saved_rows = cached[:, :, offset : offset + HEAD].reshape(x_count, y_rows * HEAD)
        grad_mixed = lax.dot_general(
            kernel.astype(jnp.bfloat16),
            grad_rows,
            (((0,), (0,)), ((), ())),
            preferred_element_type=jnp.float32,
        ).astype(jnp.bfloat16)
        coupling = lax.dot_general(
            grad_rows, saved_rows, (((1,), (1,)), ((), ())), preferred_element_type=jnp.float32
        )
        grad_query, grad_key, row_delta = local_terms(kernel, coupling, head_query, head_key)
        query_terms.append(grad_query)
        key_terms.append(grad_key)
        delta_terms.append(row_delta)
        row_slices.append(lax.dynamic_slice_in_dim(kernel, x_start, x_rows, 0))
        col_slices.append(lax.dynamic_slice_in_dim(kernel, x_start, x_rows, 1))
        mixed_heads.append(grad_mixed.reshape(x_count, y_rows, HEAD))
    mixed_rows = lax.all_to_all(
        jnp.concatenate(mixed_heads, axis=2), "slab", split_axis=0, concat_axis=1, tiled=True
    )
    x_delta_total = lax.psum(jnp.stack(delta_terms), "slab")
    query_x_grad, key_x_grad = (
        lax.psum_scatter(
            jnp.concatenate(query_terms, axis=1), "slab", scatter_dimension=0, tiled=True
        ),
        lax.psum_scatter(
            jnp.concatenate(key_terms, axis=1), "slab", scatter_dimension=0, tiled=True
        ),
    )
    query_fixes = []
    key_fixes = []
    for head_index in range(HEADS):
        offset = head_index * HEAD
        query_fix, key_fix = corrections(
            row_slices[head_index],
            col_slices[head_index],
            x_delta_total[head_index],
            query_x[:, offset : offset + HEAD],
            key_x[:, offset : offset + HEAD],
            x_start,
            x_rows,
        )
        query_fixes.append(query_fix)
        key_fixes.append(key_fix)
    query_x_grad = query_x_grad - jnp.concatenate(query_fixes, axis=1)
    key_x_grad = key_x_grad - jnp.concatenate(key_fixes, axis=1)
    value_heads = []
    query_terms = []
    key_terms = []
    delta_terms = []
    row_slices = []
    col_slices = []
    for head_index in range(HEADS):
        offset = head_index * HEAD
        head_query = query_y[:, offset : offset + HEAD]
        head_key = key_y[:, offset : offset + HEAD]
        kernel = axis_kernel(head_query, head_key)
        mixed_head = mixed_rows[:, :, offset : offset + HEAD]
        value_head = values[:, :, offset : offset + HEAD]
        grad_value = jnp.einsum(
            "jk,xje->xke",
            kernel.astype(jnp.bfloat16),
            mixed_head,
            preferred_element_type=jnp.float32,
        )
        coupling = jnp.einsum(
            "xje,xke->jk", mixed_head, value_head, preferred_element_type=jnp.float32
        )
        grad_query, grad_key, row_delta = local_terms(kernel, coupling, head_query, head_key)
        query_terms.append(grad_query)
        key_terms.append(grad_key)
        delta_terms.append(row_delta)
        row_slices.append(lax.dynamic_slice_in_dim(kernel, y_start, y_rows, 0))
        col_slices.append(lax.dynamic_slice_in_dim(kernel, y_start, y_rows, 1))
        value_heads.append(grad_value.astype(jnp.bfloat16))
    y_delta_total = lax.psum(jnp.stack(delta_terms), "slab")
    query_y_grad, key_y_grad = (
        lax.psum_scatter(
            jnp.concatenate(query_terms, axis=1), "slab", scatter_dimension=0, tiled=True
        ),
        lax.psum_scatter(
            jnp.concatenate(key_terms, axis=1), "slab", scatter_dimension=0, tiled=True
        ),
    )
    query_fixes = []
    key_fixes = []
    for head_index in range(HEADS):
        offset = head_index * HEAD
        query_fix, key_fix = corrections(
            row_slices[head_index],
            col_slices[head_index],
            y_delta_total[head_index],
            query_y[:, offset : offset + HEAD],
            key_y[:, offset : offset + HEAD],
            y_start,
            y_rows,
        )
        query_fixes.append(query_fix)
        key_fixes.append(key_fix)
    query_y_grad = query_y_grad - jnp.concatenate(query_fixes, axis=1)
    key_y_grad = key_y_grad - jnp.concatenate(key_fixes, axis=1)
    grad_values = jnp.concatenate(value_heads, axis=2)
    return (grad_values, query_x_grad, key_x_grad, query_y_grad, key_y_grad)


def gather_kernel(
    n,
    grad_hbm,
    cached_ref,
    values_ref,
    query_x_ref,
    key_x_ref,
    query_y_ref,
    key_y_ref,
    grad_values_ref,
    query_x_grad_ref,
    key_x_grad_ref,
    query_y_grad_ref,
    key_y_grad_ref,
    gathered,
    wide,
    outgoing,
    incoming,
    own_sem,
    gather_send,
    gather_recv,
    term_send,
    term_recv,
):
    me = lax.axis_index("slab")
    peers = [lax.rem(me + step, n) for step in range(1, n)]
    x_rows, y_count = values_ref.shape[0], values_ref.shape[1]
    x_count, y_rows = cached_ref.shape[0], cached_ref.shape[1]
    scale = 1.0 / math.sqrt(HEAD)

    own = pltpu.make_async_copy(grad_hbm, gathered.at[me], own_sem)
    own.start()
    barrier = pltpu.get_barrier_semaphore()
    for peer in peers:
        pl.semaphore_signal(barrier, inc=1, device_id={"slab": peer}, device_id_type=MESH)
    pl.semaphore_wait(barrier, n - 1)
    gathers = []
    for peer in reversed(peers):
        copy = pltpu.make_async_remote_copy(
            src_ref=grad_hbm,
            dst_ref=gathered.at[me],
            send_sem=gather_send.at[peer],
            recv_sem=gather_recv.at[me],
            device_id={"slab": peer},
            device_id_type=MESH,
        )
        copy.start()
        gathers.append(copy)

    query_x, kernel_x = masked_kernel(query_x_ref[...], key_x_ref[...])
    query_y, kernel_y = masked_kernel(query_y_ref[...], key_y_ref[...])
    width = x_rows * CHANNELS
    rows = lax.broadcasted_iota(jnp.int32, (x_count, width), 0)
    lanes = lax.broadcasted_iota(jnp.int32, (x_count, width), 1)
    own_columns = (rows == me * x_rows + lanes // CHANNELS).astype(jnp.bfloat16)
    spread = per_head_sum(
        jnp.dot(
            kernel_x.astype(jnp.bfloat16), own_columns, preferred_element_type=jnp.float32
        )
    )
    kernel_y_low = kernel_y.astype(jnp.bfloat16)
    cached = cached_ref[...].astype(jnp.float32)
    saved = jnp.concatenate(
        [cached[:, y, :] for y in range(y_rows)], axis=1
    ).astype(jnp.bfloat16)
    values = jnp.concatenate([values_ref[x] for x in range(x_rows)], axis=1)

    own.wait()
    for peer in peers:
        pltpu.make_async_remote_copy(
            src_ref=grad_hbm,
            dst_ref=gathered.at[peer],
            send_sem=gather_send.at[peer],
            recv_sem=gather_recv.at[peer],
            device_id={"slab": peer},
            device_id_type=MESH,
        ).wait_recv()

    mixed = [jnp.zeros((y_count, CHANNELS), jnp.float32) for _ in range(x_rows)]
    for slot in range(n):
        block = gathered[slot].astype(jnp.float32)
        wide[pl.ds(slot * x_rows * y_count, x_rows * y_count), :] = block
        for r in range(x_rows):
            i = slot * x_rows + r
            row = block[r * y_count : (r + 1) * y_count, :]
            for x in range(x_rows):
                mixed[x] += row * spread[i : i + 1, x * CHANNELS : (x + 1) * CHANNELS]
    grad_columns = jnp.concatenate(
        [
            wide[pl.ds(me * y_rows + y, x_count, stride=y_count), :]
            for y in range(y_rows)
        ],
        axis=1,
    )
    mixed = jnp.concatenate(mixed, axis=1).astype(jnp.bfloat16).astype(jnp.float32)
    mixed_heads = by_head(mixed)
    coupling_x = lax.dot_general(
        by_head(grad_columns), saved, ROWS_BY_ROWS, preferred_element_type=jnp.float32
    )
    coupling_y = lax.dot_general(
        mixed_heads, values, ROWS_BY_ROWS, preferred_element_type=jnp.float32
    )
    query_x_term, key_x_term = factor_terms(kernel_x, coupling_x, query_x, key_x_ref[...])
    query_y_term, key_y_term = factor_terms(kernel_y, coupling_y, query_y, key_y_ref[...])
    for slot in range(n):
        outgoing[slot, 0:x_rows, :] = query_x_term[slot * x_rows : (slot + 1) * x_rows]
        outgoing[slot, x_rows : 2 * x_rows, :] = key_x_term[slot * x_rows : (slot + 1) * x_rows]
        start = 2 * x_rows
        outgoing[slot, start : start + y_rows, :] = query_y_term[slot * y_rows : (slot + 1) * y_rows]
        start += y_rows
        outgoing[slot, start : start + y_rows, :] = key_y_term[slot * y_rows : (slot + 1) * y_rows]
    terms = []
    for peer in reversed(peers):
        copy = pltpu.make_async_remote_copy(
            src_ref=outgoing.at[peer],
            dst_ref=incoming.at[me],
            send_sem=term_send.at[peer],
            recv_sem=term_recv.at[me],
            device_id={"slab": peer},
            device_id_type=MESH,
        )
        copy.start()
        terms.append(copy)

    grad_values = lax.dot_general(
        kernel_y_low,
        mixed_heads,
        COLUMNS_BY_COLUMNS,
        preferred_element_type=jnp.float32,
    ).astype(grad_values_ref.dtype)
    for x in range(x_rows):
        grad_values_ref[x] = grad_values[:, x * CHANNELS : (x + 1) * CHANNELS]

    total = outgoing[me]
    for peer in peers:
        pltpu.make_async_remote_copy(
            src_ref=outgoing.at[peer],
            dst_ref=incoming.at[peer],
            send_sem=term_send.at[peer],
            recv_sem=term_recv.at[peer],
            device_id={"slab": peer},
            device_id_type=MESH,
        ).wait_recv()
        total += incoming[peer]
    total *= scale
    query_x_grad_ref[...] = total[0:x_rows]
    key_x_grad_ref[...] = total[x_rows : 2 * x_rows]
    query_y_grad_ref[...] = total[2 * x_rows : 2 * x_rows + y_rows]
    key_y_grad_ref[...] = total[2 * x_rows + y_rows : 2 * x_rows + 2 * y_rows]
    for copy in gathers + terms:
        copy.wait_send()


MESH = pl.DeviceIdType.MESH
ROWS_BY_ROWS = (((1,), (1,)), ((), ()))
COLUMNS_BY_COLUMNS = (((0,), (0,)), ((), ()))


def by_head(array):
    lanes = lax.broadcasted_iota(jnp.int32, array.shape, 1) % CHANNELS // HEAD
    return jnp.concatenate(
        [jnp.where(lanes == head, array, 0.0) for head in range(HEADS)], axis=0
    ).astype(jnp.bfloat16)


def per_head_sum(array):
    rows = array.shape[0] // HEADS
    lanes = lax.broadcasted_iota(jnp.int32, (rows, array.shape[1]), 1) % CHANNELS // HEAD
    total = array[:rows]
    for head in range(1, HEADS):
        total = jnp.where(lanes == head, array[head * rows : (head + 1) * rows], total)
    return total


def masked_kernel(queries, key_rows):
    heads = by_head(queries.astype(jnp.float32))
    scores = lax.dot_general(
        heads, key_rows, ROWS_BY_ROWS, preferred_element_type=jnp.float32
    ) / math.sqrt(HEAD)
    weights = jnp.exp(scores - jnp.max(scores, axis=1, keepdims=True))
    return heads, weights / jnp.sum(weights, axis=1, keepdims=True)


def factor_terms(kernel, coupling, queries, key_rows):
    delta = jnp.sum(kernel * coupling, axis=1, keepdims=True)
    weighted = kernel * (coupling - delta)
    high = weighted.astype(jnp.bfloat16)
    low = (weighted - high.astype(jnp.float32)).astype(jnp.bfloat16)
    query_term = jnp.dot(high, key_rows, preferred_element_type=jnp.float32) + jnp.dot(
        low, key_rows, preferred_element_type=jnp.float32
    )
    key_term = lax.dot_general(
        high, queries, COLUMNS_BY_COLUMNS, preferred_element_type=jnp.float32
    ) + lax.dot_general(low, queries, COLUMNS_BY_COLUMNS, preferred_element_type=jnp.float32)
    return per_head_sum(query_term), key_term


def gathered_form(n, grad_out, cached, values, query_x, key_x, query_y, key_y):
    x_rows, y_count = grad_out.shape[:2]
    x_count, y_rows = cached.shape[:2]
    term_rows = -(-2 * (x_rows + y_rows) // 8) * 8
    vmem = pl.BlockSpec(memory_space=pltpu.VMEM)
    return pl.pallas_call(
        functools.partial(gather_kernel, n),
        out_shape=(
            jax.ShapeDtypeStruct(values.shape, values.dtype),
            jax.ShapeDtypeStruct((x_rows, CHANNELS), jnp.float32),
            jax.ShapeDtypeStruct((x_rows, CHANNELS), jnp.float32),
            jax.ShapeDtypeStruct((y_rows, CHANNELS), jnp.float32),
            jax.ShapeDtypeStruct((y_rows, CHANNELS), jnp.float32),
        ),
        in_specs=[pl.BlockSpec(memory_space=pltpu.HBM)] + [vmem] * 6,
        out_specs=(vmem,) * 5,
        scratch_shapes=[
            pltpu.VMEM((n, x_rows * y_count, CHANNELS), jnp.bfloat16),
            pltpu.VMEM((x_count * y_count, CHANNELS), jnp.float32),
            pltpu.VMEM((n, term_rows, CHANNELS), jnp.float32),
            pltpu.VMEM((n, term_rows, CHANNELS), jnp.float32),
            pltpu.SemaphoreType.DMA,
            pltpu.SemaphoreType.DMA((n,)),
            pltpu.SemaphoreType.DMA((n,)),
            pltpu.SemaphoreType.DMA((n,)),
            pltpu.SemaphoreType.DMA((n,)),
        ],
        compiler_params=pltpu.CompilerParams(collective_id=0, has_side_effects=True),
    )(
        grad_out.reshape(x_rows * y_count, CHANNELS),
        cached,
        values,
        query_x,
        key_x,
        query_y,
        key_y,
    )


GATHERED_BYTES = 1 << 20


def on_device(n, *arrays):
    if n > 1 and arrays[0].size * arrays[0].dtype.itemsize * n <= GATHERED_BYTES:
        return gathered_form(n, *arrays)
    return exchanged_form(*arrays)


def solution(mesh):
    return jax.shard_map(
        functools.partial(on_device, mesh.shape["slab"]),
        mesh=mesh,
        in_specs=(
            P(("traj", "slab"), None, None),
            P("traj", "slab", None),
            P(("traj", "slab"), None, None),
            P("traj", None),
            P("traj", None),
            P("traj", None),
            P("traj", None),
        ),
        out_specs=(
            P(("traj", "slab"), None, None),
            P(("traj", "slab"), None),
            P(("traj", "slab"), None),
            P(("traj", "slab"), None),
            P(("traj", "slab"), None),
        ),
        check_vma=False,
    )
```

```python
import functools
import math

import jax
import jax.numpy as jnp
from jax import lax
from jax.experimental import pallas as pl
from jax.experimental.pallas import tpu as pltpu
from jax.sharding import PartitionSpec as P

HEADS = 4
HEAD = 32
CHANNELS = HEADS * HEAD


def axis_kernel(queries, key_rows):
    scores = jnp.dot(queries, key_rows.T, preferred_element_type=jnp.float32) / math.sqrt(HEAD)
    return jax.nn.softmax(scores, axis=1)


def local_terms(kernel, coupling, queries, key_rows):
    row_delta = jnp.sum(kernel * coupling, axis=1)
    weighted = kernel * coupling
    grad_query = jnp.dot(
        weighted, key_rows.astype(jnp.float32), precision=lax.Precision.HIGHEST
    ) / math.sqrt(HEAD)
    grad_key = jnp.dot(
        weighted.T, queries.astype(jnp.float32), precision=lax.Precision.HIGHEST
    ) / math.sqrt(HEAD)
    return (grad_query, grad_key, row_delta)


def corrections(own_rows, own_cols, delta_total, queries, key_rows, start, count):
    own_delta = lax.dynamic_slice_in_dim(delta_total, start, count, 0)
    query_fix = (
        own_delta[:, None]
        * jnp.dot(own_rows, key_rows.astype(jnp.float32), precision=lax.Precision.HIGHEST)
        / math.sqrt(HEAD)
    )
    key_fix = jnp.dot(
        own_cols.T,
        delta_total[:, None] * queries.astype(jnp.float32),
        precision=lax.Precision.HIGHEST,
    ) / math.sqrt(HEAD)
    return (query_fix, key_fix)


def exchanged_form(grad_out, cached, values, query_x, key_x, query_y, key_y):
    index = lax.axis_index("slab")
    x_rows = grad_out.shape[0]
    x_count = cached.shape[0]
    y_rows = cached.shape[1]
    x_start = index * x_rows
    y_start = index * y_rows
    grad_columns = lax.all_to_all(grad_out, "slab", split_axis=1, concat_axis=0, tiled=True)
    mixed_heads = []
    query_terms = []
    key_terms = []
    delta_terms = []
    row_slices = []
    col_slices = []
    for head_index in range(HEADS):
        offset = head_index * HEAD
        head_query = query_x[:, offset : offset + HEAD]
        head_key = key_x[:, offset : offset + HEAD]
        kernel = axis_kernel(head_query, head_key)
        grad_rows = grad_columns[:, :, offset : offset + HEAD].reshape(x_count, y_rows * HEAD)
        saved_rows = cached[:, :, offset : offset + HEAD].reshape(x_count, y_rows * HEAD)
        grad_mixed = lax.dot_general(
            kernel.astype(jnp.bfloat16),
            grad_rows,
            (((0,), (0,)), ((), ())),
            preferred_element_type=jnp.float32,
        ).astype(jnp.bfloat16)
        coupling = lax.dot_general(
            grad_rows, saved_rows, (((1,), (1,)), ((), ())), preferred_element_type=jnp.float32
        )
        grad_query, grad_key, row_delta = local_terms(kernel, coupling, head_query, head_key)
        query_terms.append(grad_query)
        key_terms.append(grad_key)
        delta_terms.append(row_delta)
        row_slices.append(lax.dynamic_slice_in_dim(kernel, x_start, x_rows, 0))
        col_slices.append(lax.dynamic_slice_in_dim(kernel, x_start, x_rows, 1))
        mixed_heads.append(grad_mixed.reshape(x_count, y_rows, HEAD))
    mixed_rows = lax.all_to_all(
        jnp.concatenate(mixed_heads, axis=2), "slab", split_axis=0, concat_axis=1, tiled=True
    )
    x_delta_total = lax.psum(jnp.stack(delta_terms), "slab")
    query_x_grad, key_x_grad = (
        lax.psum_scatter(
            jnp.concatenate(query_terms, axis=1), "slab", scatter_dimension=0, tiled=True
        ),
        lax.psum_scatter(
            jnp.concatenate(key_terms, axis=1), "slab", scatter_dimension=0, tiled=True
        ),
    )
    query_fixes = []
    key_fixes = []
    for head_index in range(HEADS):
        offset = head_index * HEAD
        query_fix, key_fix = corrections(
            row_slices[head_index],
            col_slices[head_index],
            x_delta_total[head_index],
            query_x[:, offset : offset + HEAD],
            key_x[:, offset : offset + HEAD],
            x_start,
            x_rows,
        )
        query_fixes.append(query_fix)
        key_fixes.append(key_fix)
    query_x_grad = query_x_grad - jnp.concatenate(query_fixes, axis=1)
    key_x_grad = key_x_grad - jnp.concatenate(key_fixes, axis=1)
    value_heads = []
    query_terms = []
    key_terms = []
    delta_terms = []
    row_slices = []
    col_slices = []
    for head_index in range(HEADS):
        offset = head_index * HEAD
        head_query = query_y[:, offset : offset + HEAD]
        head_key = key_y[:, offset : offset + HEAD]
        kernel = axis_kernel(head_query, head_key)
        mixed_head = mixed_rows[:, :, offset : offset + HEAD]
        value_head = values[:, :, offset : offset + HEAD]
        grad_value = jnp.einsum(
            "jk,xje->xke",
            kernel.astype(jnp.bfloat16),
            mixed_head,
            preferred_element_type=jnp.float32,
        )
        coupling = jnp.einsum(
            "xje,xke->jk", mixed_head, value_head, preferred_element_type=jnp.float32
        )
        grad_query, grad_key, row_delta = local_terms(kernel, coupling, head_query, head_key)
        query_terms.append(grad_query)
        key_terms.append(grad_key)
        delta_terms.append(row_delta)
        row_slices.append(lax.dynamic_slice_in_dim(kernel, y_start, y_rows, 0))
        col_slices.append(lax.dynamic_slice_in_dim(kernel, y_start, y_rows, 1))
        value_heads.append(grad_value.astype(jnp.bfloat16))
    y_delta_total = lax.psum(jnp.stack(delta_terms), "slab")
    query_y_grad, key_y_grad = (
        lax.psum_scatter(
            jnp.concatenate(query_terms, axis=1), "slab", scatter_dimension=0, tiled=True
        ),
        lax.psum_scatter(
            jnp.concatenate(key_terms, axis=1), "slab", scatter_dimension=0, tiled=True
        ),
    )
    query_fixes = []
    key_fixes = []
    for head_index in range(HEADS):
        offset = head_index * HEAD
        query_fix, key_fix = corrections(
            row_slices[head_index],
            col_slices[head_index],
            y_delta_total[head_index],
            query_y[:, offset : offset + HEAD],
            key_y[:, offset : offset + HEAD],
            y_start,
            y_rows,
        )
        query_fixes.append(query_fix)
        key_fixes.append(key_fix)
    query_y_grad = query_y_grad - jnp.concatenate(query_fixes, axis=1)
    key_y_grad = key_y_grad - jnp.concatenate(key_fixes, axis=1)
    grad_values = jnp.concatenate(value_heads, axis=2)
    return (grad_values, query_x_grad, key_x_grad, query_y_grad, key_y_grad)


MESH = pl.DeviceIdType.MESH
ROWS_BY_ROWS = (((1,), (1,)), ((), ()))


def gather_kernel(
    n,
    x_rows,
    y_rows,
    grad_hbm,
    cached_hbm,
    values_hbm,
    query_x_hbm,
    key_x_hbm,
    query_y_hbm,
    key_y_hbm,
    grad_values_ref,
    factors_ref,
    gathered,
    cached_ref,
    values_ref,
    query_x_ref,
    key_x_ref,
    query_y_ref,
    key_y_ref,
    wide,
    outgoing,
    incoming,
    own_sems,
    gather_send,
    gather_recv,
    term_send,
    term_recv,
):
    me = lax.axis_index("slab")
    peers = [lax.rem(me + step, n) for step in range(1, n)]
    x_count, y_count = query_x_ref.shape[0], query_y_ref.shape[0]

    barrier = pltpu.get_barrier_semaphore()
    for peer in peers:
        pl.semaphore_signal(barrier, inc=1, device_id={"slab": peer}, device_id_type=MESH)
    own_pairs = (
        (query_x_hbm, query_x_ref),
        (key_x_hbm, key_x_ref),
        (query_y_hbm, query_y_ref),
        (key_y_hbm, key_y_ref),
        (grad_hbm, gathered.at[me]),
        (cached_hbm, cached_ref),
        (values_hbm, values_ref),
    )
    own = [
        pltpu.make_async_copy(source, target, own_sems.at[place])
        for place, (source, target) in enumerate(own_pairs)
    ]
    for copy in own:
        copy.start()
    pl.semaphore_wait(barrier, n - 1)
    gathers = []
    for peer in reversed(peers):
        copy = pltpu.make_async_remote_copy(
            src_ref=grad_hbm,
            dst_ref=gathered.at[me],
            send_sem=gather_send.at[peer],
            recv_sem=gather_recv.at[me],
            device_id={"slab": peer},
            device_id_type=MESH,
        )
        copy.start()
        gathers.append(copy)

    for copy in own:
        copy.wait()
    key_x, key_y = key_x_ref[...], key_y_ref[...]
    query_x = by_head(query_x_ref[...].astype(jnp.float32))
    query_y = by_head(query_y_ref[...].astype(jnp.float32))
    kernel_x, kernel_x_turned = both_kernels(query_x, key_x)
    kernel_y, kernel_y_turned = both_kernels(query_y, key_y)
    width = x_rows * CHANNELS
    rows = lax.broadcasted_iota(jnp.int32, (x_count, width), 0)
    lanes = lax.broadcasted_iota(jnp.int32, (x_count, width), 1)
    own_columns = (rows == me * x_rows + lanes // CHANNELS).astype(jnp.bfloat16)
    spread = per_head(
        jnp.dot(
            kernel_x.astype(jnp.bfloat16), own_columns, preferred_element_type=jnp.float32
        )
    )
    kernel_y_low = kernel_y_turned.astype(jnp.bfloat16)
    cached = cached_ref[...].astype(jnp.float32)
    cached = jnp.concatenate(
        [cached[y * x_count : (y + 1) * x_count] for y in range(y_rows)], axis=1
    ).astype(jnp.bfloat16)
    values = values_ref[...].astype(jnp.float32)
    values = jnp.concatenate(
        [values[x * y_count : (x + 1) * y_count] for x in range(x_rows)], axis=1
    ).astype(jnp.bfloat16)

    for peer in peers:
        pltpu.make_async_remote_copy(
            src_ref=grad_hbm,
            dst_ref=gathered.at[peer],
            send_sem=gather_send.at[peer],
            recv_sem=gather_recv.at[peer],
            device_id={"slab": peer},
            device_id_type=MESH,
        ).wait_recv()

    mixed = [jnp.zeros((y_count, CHANNELS), jnp.float32) for _ in range(x_rows)]
    for slot in range(n):
        block = gathered[slot].astype(jnp.float32)
        wide[pl.ds(slot * x_rows * y_count, x_rows * y_count), :] = block
        for r in range(x_rows):
            i = slot * x_rows + r
            row = block[r * y_count : (r + 1) * y_count, :]
            for x in range(x_rows):
                mixed[x] += row * spread[i : i + 1, x * CHANNELS : (x + 1) * CHANNELS]
    grad_columns = jnp.concatenate(
        [
            wide[pl.ds(me * y_rows + y, x_count, stride=y_count), :]
            for y in range(y_rows)
        ],
        axis=1,
    )
    grad_columns = by_head(grad_columns)
    mixed = by_head(jnp.concatenate(mixed, axis=1).astype(jnp.bfloat16).astype(jnp.float32))
    query_x_term, key_x_term = factor_terms(
        kernel_x, kernel_x_turned, grad_columns, cached, query_x, key_x
    )
    query_y_term, key_y_term = factor_terms(
        kernel_y, kernel_y_turned, mixed, values, query_y, key_y
    )
    for slot in range(n):
        start = 0
        for term, count in (
            (query_x_term, x_rows),
            (key_x_term, x_rows),
            (query_y_term, y_rows),
            (key_y_term, y_rows),
        ):
            outgoing[slot, start : start + count, :] = term[slot * count : (slot + 1) * count]
            start += count
    terms = []
    for peer in reversed(peers):
        copy = pltpu.make_async_remote_copy(
            src_ref=outgoing.at[peer],
            dst_ref=incoming.at[me],
            send_sem=term_send.at[peer],
            recv_sem=term_recv.at[me],
            device_id={"slab": peer},
            device_id_type=MESH,
        )
        copy.start()
        terms.append(copy)

    grad_values = jnp.dot(kernel_y_low, mixed, preferred_element_type=jnp.float32)
    for x in range(x_rows):
        grad_values_ref[x] = grad_values[:, x * CHANNELS : (x + 1) * CHANNELS].astype(
            grad_values_ref.dtype
        )

    total = outgoing[me]
    for peer in peers:
        pltpu.make_async_remote_copy(
            src_ref=outgoing.at[peer],
            dst_ref=incoming.at[peer],
            send_sem=term_send.at[peer],
            recv_sem=term_recv.at[peer],
            device_id={"slab": peer},
            device_id_type=MESH,
        ).wait_recv()
        total += incoming[peer]
    factors_ref[...] = total * (1.0 / math.sqrt(HEAD))
    for copy in gathers + terms:
        copy.wait_send()


def by_head(array):
    lanes = lax.broadcasted_iota(jnp.int32, array.shape, 1) % CHANNELS // HEAD
    return jnp.concatenate(
        [jnp.where(lanes == head, array, 0.0) for head in range(HEADS)], axis=0
    ).astype(jnp.bfloat16)


def per_head(array):
    rows = array.shape[0] // HEADS
    lanes = lax.broadcasted_iota(jnp.int32, (rows, array.shape[1]), 1) % CHANNELS // HEAD
    picked = array[:rows]
    for head in range(1, HEADS):
        picked = jnp.where(lanes == head, array[head * rows : (head + 1) * rows], picked)
    return picked


def rows_by_rows(left, right):
    return lax.dot_general(left, right, ROWS_BY_ROWS, preferred_element_type=jnp.float32)


def both_kernels(queries, key_rows):
    kernels = []
    for scores, axis in (
        (rows_by_rows(queries, key_rows), 1),
        (rows_by_rows(key_rows, queries), 0),
    ):
        scores = scores / math.sqrt(HEAD)
        weights = jnp.exp(scores - jnp.max(scores, axis=axis, keepdims=True))
        kernels.append(weights / jnp.sum(weights, axis=axis, keepdims=True))
    return kernels


def weighted_parts(kernel, coupling, axis):
    delta = jnp.sum(kernel * coupling, axis=axis, keepdims=True)
    weighted = kernel * (coupling - delta)
    high = weighted.astype(jnp.bfloat16)
    return high, (weighted - high.astype(jnp.float32)).astype(jnp.bfloat16)


def factor_terms(kernel, kernel_turned, left, right, queries, key_rows):
    high, low = weighted_parts(kernel, rows_by_rows(left, right), 1)
    query_term = jnp.dot(high, key_rows, preferred_element_type=jnp.float32) + jnp.dot(
        low, key_rows, preferred_element_type=jnp.float32
    )
    high, low = weighted_parts(kernel_turned, rows_by_rows(right, left), 0)
    key_term = jnp.dot(high, queries, preferred_element_type=jnp.float32) + jnp.dot(
        low, queries, preferred_element_type=jnp.float32
    )
    return per_head(query_term), key_term


def hand_out_kernel(values_ref, factors_ref, *out_refs):
    out_refs[0][...] = values_ref[...]
    start = 0
    for out_ref in out_refs[1:]:
        out_ref[...] = factors_ref[start : start + out_ref.shape[0], :]
        start += out_ref.shape[0]


def gathered_form(n, grad_out, cached, values, query_x, key_x, query_y, key_y):
    x_rows, y_count = grad_out.shape[:2]
    x_count, y_rows = cached.shape[:2]
    term_rows = 2 * (x_rows + y_rows)
    vmem = pl.BlockSpec(memory_space=pltpu.VMEM)
    grad_values, factors = pl.pallas_call(
        functools.partial(gather_kernel, n, x_rows, y_rows),
        out_shape=(
            jax.ShapeDtypeStruct(values.shape, values.dtype),
            jax.ShapeDtypeStruct((term_rows, CHANNELS), jnp.float32),
        ),
        in_specs=[pl.BlockSpec(memory_space=pltpu.HBM)] * 7,
        out_specs=(vmem, vmem),
        scratch_shapes=[
            pltpu.VMEM((n, x_rows * y_count, CHANNELS), jnp.bfloat16),
            pltpu.VMEM((y_rows * x_count, CHANNELS), jnp.bfloat16),
            pltpu.VMEM((x_rows * y_count, CHANNELS), jnp.bfloat16),
            pltpu.VMEM(query_x.shape, query_x.dtype),
            pltpu.VMEM(key_x.shape, key_x.dtype),
            pltpu.VMEM(query_y.shape, query_y.dtype),
            pltpu.VMEM(key_y.shape, key_y.dtype),
            pltpu.VMEM((x_count * y_count, CHANNELS), jnp.float32),
            pltpu.VMEM((n, term_rows, CHANNELS), jnp.float32),
            pltpu.VMEM((n, term_rows, CHANNELS), jnp.float32),
            pltpu.SemaphoreType.DMA((7,)),
            pltpu.SemaphoreType.DMA((n,)),
            pltpu.SemaphoreType.DMA((n,)),
            pltpu.SemaphoreType.DMA((n,)),
            pltpu.SemaphoreType.DMA((n,)),
        ],
        compiler_params=pltpu.CompilerParams(collective_id=0, has_side_effects=True),
    )(
        grad_out.reshape(x_rows * y_count, CHANNELS),
        cached.transpose(1, 0, 2).reshape(y_rows * x_count, CHANNELS),
        values.reshape(x_rows * y_count, CHANNELS),
        query_x,
        key_x,
        query_y,
        key_y,
    )
    counts = (x_rows, x_rows, y_rows, y_rows)
    return pl.pallas_call(
        hand_out_kernel,
        out_shape=(jax.ShapeDtypeStruct(values.shape, values.dtype),)
        + tuple(jax.ShapeDtypeStruct((count, CHANNELS), jnp.float32) for count in counts),
        in_specs=[vmem] * 2,
        out_specs=(vmem,) * 5,
    )(grad_values, factors)


GATHERED_BYTES = 1 << 20


def on_device(n, *arrays):
    if n > 1 and arrays[0].size * arrays[0].dtype.itemsize * n <= GATHERED_BYTES:
        return gathered_form(n, *arrays)
    return exchanged_form(*arrays)


def solution(mesh):
    return jax.shard_map(
        functools.partial(on_device, mesh.shape["slab"]),
        mesh=mesh,
        in_specs=(
            P(("traj", "slab"), None, None),
            P("traj", "slab", None),
            P(("traj", "slab"), None, None),
            P("traj", None),
            P("traj", None),
            P("traj", None),
            P("traj", None),
        ),
        out_specs=(
            P(("traj", "slab"), None, None),
            P(("traj", "slab"), None),
            P(("traj", "slab"), None),
            P(("traj", "slab"), None),
            P(("traj", "slab"), None),
        ),
        check_vma=False,
    )
```

```python
import functools
import math

import jax
import jax.numpy as jnp
from jax import lax
from jax.experimental import pallas as pl
from jax.experimental.pallas import tpu as pltpu
from jax.sharding import PartitionSpec as P

HEADS = 4
HEAD = 32
CHANNELS = HEADS * HEAD


def axis_kernel(queries, key_rows):
    scores = jnp.dot(queries, key_rows.T, preferred_element_type=jnp.float32) / math.sqrt(HEAD)
    return jax.nn.softmax(scores, axis=1)


def local_terms(kernel, coupling, queries, key_rows):
    row_delta = jnp.sum(kernel * coupling, axis=1)
    weighted = kernel * coupling
    grad_query = jnp.dot(
        weighted, key_rows.astype(jnp.float32), precision=lax.Precision.HIGHEST
    ) / math.sqrt(HEAD)
    grad_key = jnp.dot(
        weighted.T, queries.astype(jnp.float32), precision=lax.Precision.HIGHEST
    ) / math.sqrt(HEAD)
    return (grad_query, grad_key, row_delta)


def corrections(own_rows, own_cols, delta_total, queries, key_rows, start, count):
    own_delta = lax.dynamic_slice_in_dim(delta_total, start, count, 0)
    query_fix = (
        own_delta[:, None]
        * jnp.dot(own_rows, key_rows.astype(jnp.float32), precision=lax.Precision.HIGHEST)
        / math.sqrt(HEAD)
    )
    key_fix = jnp.dot(
        own_cols.T,
        delta_total[:, None] * queries.astype(jnp.float32),
        precision=lax.Precision.HIGHEST,
    ) / math.sqrt(HEAD)
    return (query_fix, key_fix)


def exchanged_form(grad_out, cached, values, query_x, key_x, query_y, key_y):
    index = lax.axis_index("slab")
    x_rows = grad_out.shape[0]
    x_count = cached.shape[0]
    y_rows = cached.shape[1]
    x_start = index * x_rows
    y_start = index * y_rows
    grad_columns = lax.all_to_all(grad_out, "slab", split_axis=1, concat_axis=0, tiled=True)
    mixed_heads = []
    query_terms = []
    key_terms = []
    delta_terms = []
    row_slices = []
    col_slices = []
    for head_index in range(HEADS):
        offset = head_index * HEAD
        head_query = query_x[:, offset : offset + HEAD]
        head_key = key_x[:, offset : offset + HEAD]
        kernel = axis_kernel(head_query, head_key)
        grad_rows = grad_columns[:, :, offset : offset + HEAD].reshape(x_count, y_rows * HEAD)
        saved_rows = cached[:, :, offset : offset + HEAD].reshape(x_count, y_rows * HEAD)
        grad_mixed = lax.dot_general(
            kernel.astype(jnp.bfloat16),
            grad_rows,
            (((0,), (0,)), ((), ())),
            preferred_element_type=jnp.float32,
        ).astype(jnp.bfloat16)
        coupling = lax.dot_general(
            grad_rows, saved_rows, (((1,), (1,)), ((), ())), preferred_element_type=jnp.float32
        )
        grad_query, grad_key, row_delta = local_terms(kernel, coupling, head_query, head_key)
        query_terms.append(grad_query)
        key_terms.append(grad_key)
        delta_terms.append(row_delta)
        row_slices.append(lax.dynamic_slice_in_dim(kernel, x_start, x_rows, 0))
        col_slices.append(lax.dynamic_slice_in_dim(kernel, x_start, x_rows, 1))
        mixed_heads.append(grad_mixed.reshape(x_count, y_rows, HEAD))
    mixed_rows = lax.all_to_all(
        jnp.concatenate(mixed_heads, axis=2), "slab", split_axis=0, concat_axis=1, tiled=True
    )
    x_delta_total = lax.psum(jnp.stack(delta_terms), "slab")
    query_x_grad, key_x_grad = (
        lax.psum_scatter(
            jnp.concatenate(query_terms, axis=1), "slab", scatter_dimension=0, tiled=True
        ),
        lax.psum_scatter(
            jnp.concatenate(key_terms, axis=1), "slab", scatter_dimension=0, tiled=True
        ),
    )
    query_fixes = []
    key_fixes = []
    for head_index in range(HEADS):
        offset = head_index * HEAD
        query_fix, key_fix = corrections(
            row_slices[head_index],
            col_slices[head_index],
            x_delta_total[head_index],
            query_x[:, offset : offset + HEAD],
            key_x[:, offset : offset + HEAD],
            x_start,
            x_rows,
        )
        query_fixes.append(query_fix)
        key_fixes.append(key_fix)
    query_x_grad = query_x_grad - jnp.concatenate(query_fixes, axis=1)
    key_x_grad = key_x_grad - jnp.concatenate(key_fixes, axis=1)
    value_heads = []
    query_terms = []
    key_terms = []
    delta_terms = []
    row_slices = []
    col_slices = []
    for head_index in range(HEADS):
        offset = head_index * HEAD
        head_query = query_y[:, offset : offset + HEAD]
        head_key = key_y[:, offset : offset + HEAD]
        kernel = axis_kernel(head_query, head_key)
        mixed_head = mixed_rows[:, :, offset : offset + HEAD]
        value_head = values[:, :, offset : offset + HEAD]
        grad_value = jnp.einsum(
            "jk,xje->xke",
            kernel.astype(jnp.bfloat16),
            mixed_head,
            preferred_element_type=jnp.float32,
        )
        coupling = jnp.einsum(
            "xje,xke->jk", mixed_head, value_head, preferred_element_type=jnp.float32
        )
        grad_query, grad_key, row_delta = local_terms(kernel, coupling, head_query, head_key)
        query_terms.append(grad_query)
        key_terms.append(grad_key)
        delta_terms.append(row_delta)
        row_slices.append(lax.dynamic_slice_in_dim(kernel, y_start, y_rows, 0))
        col_slices.append(lax.dynamic_slice_in_dim(kernel, y_start, y_rows, 1))
        value_heads.append(grad_value.astype(jnp.bfloat16))
    y_delta_total = lax.psum(jnp.stack(delta_terms), "slab")
    query_y_grad, key_y_grad = (
        lax.psum_scatter(
            jnp.concatenate(query_terms, axis=1), "slab", scatter_dimension=0, tiled=True
        ),
        lax.psum_scatter(
            jnp.concatenate(key_terms, axis=1), "slab", scatter_dimension=0, tiled=True
        ),
    )
    query_fixes = []
    key_fixes = []
    for head_index in range(HEADS):
        offset = head_index * HEAD
        query_fix, key_fix = corrections(
            row_slices[head_index],
            col_slices[head_index],
            y_delta_total[head_index],
            query_y[:, offset : offset + HEAD],
            key_y[:, offset : offset + HEAD],
            y_start,
            y_rows,
        )
        query_fixes.append(query_fix)
        key_fixes.append(key_fix)
    query_y_grad = query_y_grad - jnp.concatenate(query_fixes, axis=1)
    key_y_grad = key_y_grad - jnp.concatenate(key_fixes, axis=1)
    grad_values = jnp.concatenate(value_heads, axis=2)
    return (grad_values, query_x_grad, key_x_grad, query_y_grad, key_y_grad)


MESH = pl.DeviceIdType.MESH
ROWS_BY_ROWS = (((1,), (1,)), ((), ()))


def gather_kernel(
    n,
    x_rows,
    y_rows,
    grad_hbm,
    cached_hbm,
    values_hbm,
    query_x_hbm,
    key_x_hbm,
    query_y_hbm,
    key_y_hbm,
    grad_values_ref,
    factors_ref,
    gathered,
    cached_ref,
    values_ref,
    query_x_ref,
    key_x_ref,
    query_y_ref,
    key_y_ref,
    spread,
    wide,
    outgoing,
    incoming,
    own_sems,
    gather_send,
    gather_recv,
    term_send,
    term_recv,
):
    me = lax.axis_index("slab")
    peers = [
        lax.rem(me + step, n) for step in sorted(range(1, n), key=lambda s: abs(2 * s - n))
    ]
    x_count, y_count = query_x_ref.shape[0], query_y_ref.shape[0]

    own_grad = pltpu.make_async_copy(grad_hbm, gathered.at[me], own_sems.at[6])
    own_grad.start()
    barrier = pltpu.get_barrier_semaphore()
    for peer in peers:
        pl.semaphore_signal(barrier, inc=1, device_id={"slab": peer}, device_id_type=MESH)
    own_pairs = (
        (query_x_hbm, query_x_ref),
        (key_x_hbm, key_x_ref),
        (query_y_hbm, query_y_ref),
        (key_y_hbm, key_y_ref),
        (cached_hbm, cached_ref),
        (values_hbm, values_ref),
    )
    own = [
        pltpu.make_async_copy(source, target, own_sems.at[place])
        for place, (source, target) in enumerate(own_pairs)
    ]
    for copy in own:
        copy.start()
    own_grad.wait()
    pl.semaphore_wait(barrier, n - 1)
    gathers = []
    for peer in peers:
        copy = pltpu.make_async_remote_copy(
            src_ref=gathered.at[me],
            dst_ref=gathered.at[me],
            send_sem=gather_send.at[peer],
            recv_sem=gather_recv.at[me],
            device_id={"slab": peer},
            device_id_type=MESH,
        )
        copy.start()
        gathers.append(copy)

    for copy in own:
        copy.wait()
    key_x, key_y = key_x_ref[...], key_y_ref[...]
    query_x = by_head(query_x_ref[...].astype(jnp.float32))
    query_y = by_head(query_y_ref[...].astype(jnp.float32))
    kernel_x, kernel_x_turned = both_kernels(query_x, key_x)
    kernel_y, kernel_y_turned = both_kernels(query_y, key_y)
    width = x_rows * CHANNELS
    rows = lax.broadcasted_iota(jnp.int32, (x_count, width), 0)
    lanes = lax.broadcasted_iota(jnp.int32, (x_count, width), 1)
    own_columns = (rows == me * x_rows + lanes // CHANNELS).astype(jnp.bfloat16)
    spread[...] = per_head(
        jnp.dot(
            kernel_x.astype(jnp.bfloat16), own_columns, preferred_element_type=jnp.float32
        )
    )
    kernel_y_low = kernel_y_turned.astype(jnp.bfloat16)
    cached = cached_ref[...].astype(jnp.float32)
    cached = jnp.concatenate(
        [cached[y * x_count : (y + 1) * x_count] for y in range(y_rows)], axis=1
    ).astype(jnp.bfloat16)
    values = values_ref[...].astype(jnp.float32)
    values = jnp.concatenate(
        [values[x * y_count : (x + 1) * y_count] for x in range(x_rows)], axis=1
    ).astype(jnp.bfloat16)

    mixed = [jnp.zeros((y_count, CHANNELS), jnp.float32) for _ in range(x_rows)]
    for slot in [me] + peers[::-1]:
        if slot is not me:
            pltpu.make_async_remote_copy(
                src_ref=gathered.at[me],
                dst_ref=gathered.at[slot],
                send_sem=gather_send.at[slot],
                recv_sem=gather_recv.at[slot],
                device_id={"slab": slot},
                device_id_type=MESH,
            ).wait_recv()
        block = gathered[slot].astype(jnp.float32)
        rows = x_rows * y_count
        wide[pl.ds(pl.multiple_of(slot * rows, 8), rows), :] = block
        for r in range(x_rows):
            row = block[r * y_count : (r + 1) * y_count, :]
            factor = spread[pl.ds(slot * x_rows + r, 1), :]
            for x in range(x_rows):
                mixed[x] += row * factor[:, x * CHANNELS : (x + 1) * CHANNELS]
    grad_columns = jnp.concatenate(
        [
            wide[pl.ds(me * y_rows + y, x_count, stride=y_count), :]
            for y in range(y_rows)
        ],
        axis=1,
    )
    grad_columns = by_head(grad_columns)
    mixed = by_head(jnp.concatenate(mixed, axis=1).astype(jnp.bfloat16).astype(jnp.float32))
    query_x_term, key_x_term = factor_terms(
        kernel_x, kernel_x_turned, grad_columns, cached, query_x, key_x
    )
    query_y_term, key_y_term = factor_terms(
        kernel_y, kernel_y_turned, mixed, values, query_y, key_y
    )
    for slot in range(n):
        start = 0
        for term, count in (
            (query_x_term, x_rows),
            (key_x_term, x_rows),
            (query_y_term, y_rows),
            (key_y_term, y_rows),
        ):
            outgoing[slot, start : start + count, :] = term[slot * count : (slot + 1) * count]
            start += count
    terms = []
    for peer in peers:
        copy = pltpu.make_async_remote_copy(
            src_ref=outgoing.at[peer],
            dst_ref=incoming.at[me],
            send_sem=term_send.at[peer],
            recv_sem=term_recv.at[me],
            device_id={"slab": peer},
            device_id_type=MESH,
        )
        copy.start()
        terms.append(copy)

    grad_values = jnp.dot(kernel_y_low, mixed, preferred_element_type=jnp.float32)
    for x in range(x_rows):
        grad_values_ref[x] = grad_values[:, x * CHANNELS : (x + 1) * CHANNELS].astype(
            grad_values_ref.dtype
        )

    total = outgoing[me]
    for peer in peers[::-1]:
        pltpu.make_async_remote_copy(
            src_ref=outgoing.at[peer],
            dst_ref=incoming.at[peer],
            send_sem=term_send.at[peer],
            recv_sem=term_recv.at[peer],
            device_id={"slab": peer},
            device_id_type=MESH,
        ).wait_recv()
        total += incoming[peer]
    factors_ref[...] = total * (1.0 / math.sqrt(HEAD))
    for copy in gathers + terms:
        copy.wait_send()


def by_head(array):
    lanes = lax.broadcasted_iota(jnp.int32, array.shape, 1) % CHANNELS // HEAD
    return jnp.concatenate(
        [jnp.where(lanes == head, array, 0.0) for head in range(HEADS)], axis=0
    ).astype(jnp.bfloat16)


def per_head(array):
    rows = array.shape[0] // HEADS
    lanes = lax.broadcasted_iota(jnp.int32, (rows, array.shape[1]), 1) % CHANNELS // HEAD
    picked = array[:rows]
    for head in range(1, HEADS):
        picked = jnp.where(lanes == head, array[head * rows : (head + 1) * rows], picked)
    return picked


def rows_by_rows(left, right):
    return lax.dot_general(left, right, ROWS_BY_ROWS, preferred_element_type=jnp.float32)


def both_kernels(queries, key_rows):
    kernels = []
    for scores, axis in (
        (rows_by_rows(queries, key_rows), 1),
        (rows_by_rows(key_rows, queries), 0),
    ):
        scores = scores / math.sqrt(HEAD)
        weights = jnp.exp(scores - jnp.max(scores, axis=axis, keepdims=True))
        kernels.append(weights / jnp.sum(weights, axis=axis, keepdims=True))
    return kernels


def weighted_parts(kernel, coupling, axis):
    delta = jnp.sum(kernel * coupling, axis=axis, keepdims=True)
    weighted = kernel * (coupling - delta)
    high = weighted.astype(jnp.bfloat16)
    return high, (weighted - high.astype(jnp.float32)).astype(jnp.bfloat16)


def factor_terms(kernel, kernel_turned, left, right, queries, key_rows):
    high, low = weighted_parts(kernel, rows_by_rows(left, right), 1)
    query_term = jnp.dot(high, key_rows, preferred_element_type=jnp.float32) + jnp.dot(
        low, key_rows, preferred_element_type=jnp.float32
    )
    high, low = weighted_parts(kernel_turned, rows_by_rows(right, left), 0)
    key_term = jnp.dot(high, queries, preferred_element_type=jnp.float32) + jnp.dot(
        low, queries, preferred_element_type=jnp.float32
    )
    return per_head(query_term), key_term


def hand_out_kernel(values_ref, factors_ref, *out_refs):
    out_refs[0][...] = values_ref[...]
    start = 0
    for out_ref in out_refs[1:]:
        out_ref[...] = factors_ref[start : start + out_ref.shape[0], :]
        start += out_ref.shape[0]


def gathered_form(n, grad_out, cached, values, query_x, key_x, query_y, key_y):
    x_rows, y_count = grad_out.shape[:2]
    x_count, y_rows = cached.shape[:2]
    term_rows = 2 * (x_rows + y_rows)
    vmem = pl.BlockSpec(memory_space=pltpu.VMEM)
    grad_values, factors = pl.pallas_call(
        functools.partial(gather_kernel, n, x_rows, y_rows),
        out_shape=(
            pltpu.VMEM(values.shape, values.dtype),
            pltpu.VMEM((term_rows, CHANNELS), jnp.float32),
        ),
        in_specs=[pl.BlockSpec(memory_space=pltpu.HBM)] * 7,
        out_specs=(vmem, vmem),
        scratch_shapes=[
            pltpu.VMEM((n, x_rows * y_count, CHANNELS), jnp.bfloat16),
            pltpu.VMEM((y_rows * x_count, CHANNELS), jnp.bfloat16),
            pltpu.VMEM((x_rows * y_count, CHANNELS), jnp.bfloat16),
            pltpu.VMEM(query_x.shape, query_x.dtype),
            pltpu.VMEM(key_x.shape, key_x.dtype),
            pltpu.VMEM(query_y.shape, query_y.dtype),
            pltpu.VMEM(key_y.shape, key_y.dtype),
            pltpu.VMEM((x_count, x_rows * CHANNELS), jnp.float32),
            pltpu.VMEM((x_count * y_count, CHANNELS), jnp.float32),
            pltpu.VMEM((n, term_rows, CHANNELS), jnp.float32),
            pltpu.VMEM((n, term_rows, CHANNELS), jnp.float32),
            pltpu.SemaphoreType.DMA((7,)),
            pltpu.SemaphoreType.DMA((n,)),
            pltpu.SemaphoreType.DMA((n,)),
            pltpu.SemaphoreType.DMA((n,)),
            pltpu.SemaphoreType.DMA((n,)),
        ],
        compiler_params=pltpu.CompilerParams(
            collective_id=0, has_side_effects=True, vmem_limit_bytes=KERNEL_BYTES
        ),
    )(
        *(
            pltpu.with_memory_space_constraint(array, pltpu.HBM)
            for array in (
                grad_out.reshape(x_rows * y_count, CHANNELS),
                cached.transpose(1, 0, 2).reshape(y_rows * x_count, CHANNELS),
                values.reshape(x_rows * y_count, CHANNELS),
                query_x,
                key_x,
                query_y,
                key_y,
            )
        )
    )
    counts = (x_rows, x_rows, y_rows, y_rows)
    return pl.pallas_call(
        hand_out_kernel,
        out_shape=(jax.ShapeDtypeStruct(values.shape, values.dtype),)
        + tuple(jax.ShapeDtypeStruct((count, CHANNELS), jnp.float32) for count in counts),
        in_specs=[vmem] * 2,
        out_specs=(vmem,) * 5,
        compiler_params=pltpu.CompilerParams(vmem_limit_bytes=KERNEL_BYTES),
    )(grad_values, factors)


GATHERED_BYTES = 1 << 20
KERNEL_BYTES = 16 << 20


def on_device(n, *arrays):
    if n > 1 and arrays[0].size * arrays[0].dtype.itemsize * n <= GATHERED_BYTES:
        return gathered_form(n, *arrays)
    return exchanged_form(*arrays)


def solution(mesh):
    return jax.shard_map(
        functools.partial(on_device, mesh.shape["slab"]),
        mesh=mesh,
        in_specs=(
            P(("traj", "slab"), None, None),
            P("traj", "slab", None),
            P(("traj", "slab"), None, None),
            P("traj", None),
            P("traj", None),
            P("traj", None),
            P("traj", None),
        ),
        out_specs=(
            P(("traj", "slab"), None, None),
            P(("traj", "slab"), None),
            P(("traj", "slab"), None),
            P(("traj", "slab"), None),
            P(("traj", "slab"), None),
        ),
        check_vma=False,
    )
```

```python
import functools
import math

import jax
import jax.numpy as jnp
from jax import lax
from jax.experimental import pallas as pl
from jax.experimental.pallas import tpu as pltpu
from jax.sharding import PartitionSpec as P

HEADS = 4
HEAD = 32
CHANNELS = HEADS * HEAD


def axis_kernel(queries, key_rows):
    scores = jnp.dot(queries, key_rows.T, preferred_element_type=jnp.float32) / math.sqrt(HEAD)
    return jax.nn.softmax(scores, axis=1)


def local_terms(kernel, coupling, queries, key_rows):
    row_delta = jnp.sum(kernel * coupling, axis=1)
    weighted = kernel * coupling
    grad_query = jnp.dot(
        weighted, key_rows.astype(jnp.float32), precision=lax.Precision.HIGHEST
    ) / math.sqrt(HEAD)
    grad_key = jnp.dot(
        weighted.T, queries.astype(jnp.float32), precision=lax.Precision.HIGHEST
    ) / math.sqrt(HEAD)
    return (grad_query, grad_key, row_delta)


def corrections(own_rows, own_cols, delta_total, queries, key_rows, start, count):
    own_delta = lax.dynamic_slice_in_dim(delta_total, start, count, 0)
    query_fix = (
        own_delta[:, None]
        * jnp.dot(own_rows, key_rows.astype(jnp.float32), precision=lax.Precision.HIGHEST)
        / math.sqrt(HEAD)
    )
    key_fix = jnp.dot(
        own_cols.T,
        delta_total[:, None] * queries.astype(jnp.float32),
        precision=lax.Precision.HIGHEST,
    ) / math.sqrt(HEAD)
    return (query_fix, key_fix)


def exchanged_form(grad_out, cached, values, query_x, key_x, query_y, key_y):
    index = lax.axis_index("slab")
    x_rows = grad_out.shape[0]
    x_count = cached.shape[0]
    y_rows = cached.shape[1]
    x_start = index * x_rows
    y_start = index * y_rows
    grad_columns = lax.all_to_all(grad_out, "slab", split_axis=1, concat_axis=0, tiled=True)
    mixed_heads = []
    query_terms = []
    key_terms = []
    delta_terms = []
    row_slices = []
    col_slices = []
    for head_index in range(HEADS):
        offset = head_index * HEAD
        head_query = query_x[:, offset : offset + HEAD]
        head_key = key_x[:, offset : offset + HEAD]
        kernel = axis_kernel(head_query, head_key)
        grad_rows = grad_columns[:, :, offset : offset + HEAD].reshape(x_count, y_rows * HEAD)
        saved_rows = cached[:, :, offset : offset + HEAD].reshape(x_count, y_rows * HEAD)
        grad_mixed = lax.dot_general(
            kernel.astype(jnp.bfloat16),
            grad_rows,
            (((0,), (0,)), ((), ())),
            preferred_element_type=jnp.float32,
        ).astype(jnp.bfloat16)
        coupling = lax.dot_general(
            grad_rows, saved_rows, (((1,), (1,)), ((), ())), preferred_element_type=jnp.float32
        )
        grad_query, grad_key, row_delta = local_terms(kernel, coupling, head_query, head_key)
        query_terms.append(grad_query)
        key_terms.append(grad_key)
        delta_terms.append(row_delta)
        row_slices.append(lax.dynamic_slice_in_dim(kernel, x_start, x_rows, 0))
        col_slices.append(lax.dynamic_slice_in_dim(kernel, x_start, x_rows, 1))
        mixed_heads.append(grad_mixed.reshape(x_count, y_rows, HEAD))
    mixed_rows = lax.all_to_all(
        jnp.concatenate(mixed_heads, axis=2), "slab", split_axis=0, concat_axis=1, tiled=True
    )
    x_delta_total = lax.psum(jnp.stack(delta_terms), "slab")
    query_x_grad, key_x_grad = (
        lax.psum_scatter(
            jnp.concatenate(query_terms, axis=1), "slab", scatter_dimension=0, tiled=True
        ),
        lax.psum_scatter(
            jnp.concatenate(key_terms, axis=1), "slab", scatter_dimension=0, tiled=True
        ),
    )
    query_fixes = []
    key_fixes = []
    for head_index in range(HEADS):
        offset = head_index * HEAD
        query_fix, key_fix = corrections(
            row_slices[head_index],
            col_slices[head_index],
            x_delta_total[head_index],
            query_x[:, offset : offset + HEAD],
            key_x[:, offset : offset + HEAD],
            x_start,
            x_rows,
        )
        query_fixes.append(query_fix)
        key_fixes.append(key_fix)
    query_x_grad = query_x_grad - jnp.concatenate(query_fixes, axis=1)
    key_x_grad = key_x_grad - jnp.concatenate(key_fixes, axis=1)
    value_heads = []
    query_terms = []
    key_terms = []
    delta_terms = []
    row_slices = []
    col_slices = []
    for head_index in range(HEADS):
        offset = head_index * HEAD
        head_query = query_y[:, offset : offset + HEAD]
        head_key = key_y[:, offset : offset + HEAD]
        kernel = axis_kernel(head_query, head_key)
        mixed_head = mixed_rows[:, :, offset : offset + HEAD]
        value_head = values[:, :, offset : offset + HEAD]
        grad_value = jnp.einsum(
            "jk,xje->xke",
            kernel.astype(jnp.bfloat16),
            mixed_head,
            preferred_element_type=jnp.float32,
        )
        coupling = jnp.einsum(
            "xje,xke->jk", mixed_head, value_head, preferred_element_type=jnp.float32
        )
        grad_query, grad_key, row_delta = local_terms(kernel, coupling, head_query, head_key)
        query_terms.append(grad_query)
        key_terms.append(grad_key)
        delta_terms.append(row_delta)
        row_slices.append(lax.dynamic_slice_in_dim(kernel, y_start, y_rows, 0))
        col_slices.append(lax.dynamic_slice_in_dim(kernel, y_start, y_rows, 1))
        value_heads.append(grad_value.astype(jnp.bfloat16))
    y_delta_total = lax.psum(jnp.stack(delta_terms), "slab")
    query_y_grad, key_y_grad = (
        lax.psum_scatter(
            jnp.concatenate(query_terms, axis=1), "slab", scatter_dimension=0, tiled=True
        ),
        lax.psum_scatter(
            jnp.concatenate(key_terms, axis=1), "slab", scatter_dimension=0, tiled=True
        ),
    )
    query_fixes = []
    key_fixes = []
    for head_index in range(HEADS):
        offset = head_index * HEAD
        query_fix, key_fix = corrections(
            row_slices[head_index],
            col_slices[head_index],
            y_delta_total[head_index],
            query_y[:, offset : offset + HEAD],
            key_y[:, offset : offset + HEAD],
            y_start,
            y_rows,
        )
        query_fixes.append(query_fix)
        key_fixes.append(key_fix)
    query_y_grad = query_y_grad - jnp.concatenate(query_fixes, axis=1)
    key_y_grad = key_y_grad - jnp.concatenate(key_fixes, axis=1)
    grad_values = jnp.concatenate(value_heads, axis=2)
    return (grad_values, query_x_grad, key_x_grad, query_y_grad, key_y_grad)


MESH = pl.DeviceIdType.MESH
ROWS_BY_ROWS = (((1,), (1,)), ((), ()))


def gather_kernel(
    n,
    x_rows,
    y_rows,
    grad_hbm,
    cached_hbm,
    values_hbm,
    query_x_hbm,
    key_x_hbm,
    query_y_hbm,
    key_y_hbm,
    grad_values_ref,
    factors_ref,
    gathered,
    cached_ref,
    values_ref,
    query_x_ref,
    key_x_ref,
    query_y_ref,
    key_y_ref,
    spread,
    wide,
    outgoing,
    incoming,
    own_sems,
    gather_send,
    gather_recv,
    term_send,
    term_recv,
):
    me = lax.axis_index("slab")
    peers = [
        lax.rem(me + step, n) for step in sorted(range(1, n), key=lambda s: abs(2 * s - n))
    ]
    mate = me + 1 - 2 * lax.rem(me, 2)
    far = [
        lax.rem(me + step, n) for step in sorted(range(2, n, 2), key=lambda s: abs(2 * s - n))
    ]
    x_count, y_count = query_x_ref.shape[0], query_y_ref.shape[0]

    own_grad = pltpu.make_async_copy(grad_hbm, gathered.at[me], own_sems.at[6])
    own_grad.start()
    barrier = pltpu.get_barrier_semaphore()
    for peer in peers:
        pl.semaphore_signal(barrier, inc=1, device_id={"slab": peer}, device_id_type=MESH)
    own_pairs = (
        (query_x_hbm, query_x_ref),
        (key_x_hbm, key_x_ref),
        (query_y_hbm, query_y_ref),
        (key_y_hbm, key_y_ref),
        (cached_hbm, cached_ref),
        (values_hbm, values_ref),
    )
    own = [
        pltpu.make_async_copy(source, target, own_sems.at[place])
        for place, (source, target) in enumerate(own_pairs)
    ]
    for copy in own:
        copy.start()
    own_grad.wait()
    pl.semaphore_wait(barrier, n - 1)
    def block_copy(block, target):
        return pltpu.make_async_remote_copy(
            src_ref=gathered.at[block],
            dst_ref=gathered.at[block],
            send_sem=gather_send.at[target, block],
            recv_sem=gather_recv.at[block],
            device_id={"slab": target},
            device_id_type=MESH,
        )

    gathers = [block_copy(me, target) for target in far + [mate]]
    for copy in gathers:
        copy.start()

    for copy in own:
        copy.wait()
    key_x, key_y = key_x_ref[...], key_y_ref[...]
    query_x = by_head(query_x_ref[...].astype(jnp.float32))
    query_y = by_head(query_y_ref[...].astype(jnp.float32))
    kernel_x, kernel_x_turned = both_kernels(query_x, key_x)
    kernel_y, kernel_y_turned = both_kernels(query_y, key_y)
    width = x_rows * CHANNELS
    rows = lax.broadcasted_iota(jnp.int32, (x_count, width), 0)
    lanes = lax.broadcasted_iota(jnp.int32, (x_count, width), 1)
    own_columns = (rows == me * x_rows + lanes // CHANNELS).astype(jnp.bfloat16)
    spread[...] = per_head(
        jnp.dot(
            kernel_x.astype(jnp.bfloat16), own_columns, preferred_element_type=jnp.float32
        )
    )
    kernel_y_low = kernel_y_turned.astype(jnp.bfloat16)
    cached = cached_ref[...].astype(jnp.float32)
    cached = jnp.concatenate(
        [cached[y * x_count : (y + 1) * x_count] for y in range(y_rows)], axis=1
    ).astype(jnp.bfloat16)
    values = values_ref[...].astype(jnp.float32)
    values = jnp.concatenate(
        [values[x * y_count : (x + 1) * y_count] for x in range(x_rows)], axis=1
    ).astype(jnp.bfloat16)

    mixed = [jnp.zeros((y_count, CHANNELS), jnp.float32) for _ in range(x_rows)]
    handed = [lax.rem(mate + step, n) for step in range(2, n, 2)]
    for slot in [me, mate] + far[::-1] + handed:
        if slot is not me:
            block_copy(slot, mate).wait_recv()
        if any(slot is other for other in far):
            copy = block_copy(slot, mate)
            copy.start()
            gathers.append(copy)
        block = gathered[slot].astype(jnp.float32)
        rows = x_rows * y_count
        wide[pl.ds(pl.multiple_of(slot * rows, 8), rows), :] = block
        for r in range(x_rows):
            row = block[r * y_count : (r + 1) * y_count, :]
            factor = spread[pl.ds(slot * x_rows + r, 1), :]
            for x in range(x_rows):
                mixed[x] += row * factor[:, x * CHANNELS : (x + 1) * CHANNELS]
    grad_columns = jnp.concatenate(
        [
            wide[pl.ds(me * y_rows + y, x_count, stride=y_count), :]
            for y in range(y_rows)
        ],
        axis=1,
    )
    grad_columns = by_head(grad_columns)
    mixed = by_head(jnp.concatenate(mixed, axis=1).astype(jnp.bfloat16).astype(jnp.float32))
    query_x_term, key_x_term = factor_terms(
        kernel_x, kernel_x_turned, grad_columns, cached, query_x, key_x
    )
    query_y_term, key_y_term = factor_terms(
        kernel_y, kernel_y_turned, mixed, values, query_y, key_y
    )
    for slot in range(n):
        start = 0
        for term, count in (
            (query_x_term, x_rows),
            (key_x_term, x_rows),
            (query_y_term, y_rows),
            (key_y_term, y_rows),
        ):
            outgoing[slot, start : start + count, :] = term[slot * count : (slot + 1) * count]
            start += count
    terms = []
    for peer in peers:
        copy = pltpu.make_async_remote_copy(
            src_ref=outgoing.at[peer],
            dst_ref=incoming.at[me],
            send_sem=term_send.at[peer],
            recv_sem=term_recv.at[me],
            device_id={"slab": peer},
            device_id_type=MESH,
        )
        copy.start()
        terms.append(copy)

    grad_values = jnp.dot(kernel_y_low, mixed, preferred_element_type=jnp.float32)
    for x in range(x_rows):
        grad_values_ref[x] = grad_values[:, x * CHANNELS : (x + 1) * CHANNELS].astype(
            grad_values_ref.dtype
        )

    total = outgoing[me]
    for peer in peers[::-1]:
        pltpu.make_async_remote_copy(
            src_ref=outgoing.at[peer],
            dst_ref=incoming.at[peer],
            send_sem=term_send.at[peer],
            recv_sem=term_recv.at[peer],
            device_id={"slab": peer},
            device_id_type=MESH,
        ).wait_recv()
        total += incoming[peer]
    factors_ref[...] = total * (1.0 / math.sqrt(HEAD))
    for copy in gathers + terms:
        copy.wait_send()


def by_head(array):
    lanes = lax.broadcasted_iota(jnp.int32, array.shape, 1) % CHANNELS // HEAD
    return jnp.concatenate(
        [jnp.where(lanes == head, array, 0.0) for head in range(HEADS)], axis=0
    ).astype(jnp.bfloat16)


def per_head(array):
    rows = array.shape[0] // HEADS
    lanes = lax.broadcasted_iota(jnp.int32, (rows, array.shape[1]), 1) % CHANNELS // HEAD
    picked = array[:rows]
    for head in range(1, HEADS):
        picked = jnp.where(lanes == head, array[head * rows : (head + 1) * rows], picked)
    return picked


def rows_by_rows(left, right):
    return lax.dot_general(left, right, ROWS_BY_ROWS, preferred_element_type=jnp.float32)


def both_kernels(queries, key_rows):
    kernels = []
    for scores, axis in (
        (rows_by_rows(queries, key_rows), 1),
        (rows_by_rows(key_rows, queries), 0),
    ):
        scores = scores / math.sqrt(HEAD)
        weights = jnp.exp(scores - jnp.max(scores, axis=axis, keepdims=True))
        kernels.append(weights / jnp.sum(weights, axis=axis, keepdims=True))
    return kernels


def weighted_parts(kernel, coupling, axis):
    delta = jnp.sum(kernel * coupling, axis=axis, keepdims=True)
    weighted = kernel * (coupling - delta)
    high = weighted.astype(jnp.bfloat16)
    return high, (weighted - high.astype(jnp.float32)).astype(jnp.bfloat16)


def factor_terms(kernel, kernel_turned, left, right, queries, key_rows):
    high, low = weighted_parts(kernel, rows_by_rows(left, right), 1)
    query_term = jnp.dot(high, key_rows, preferred_element_type=jnp.float32) + jnp.dot(
        low, key_rows, preferred_element_type=jnp.float32
    )
    high, low = weighted_parts(kernel_turned, rows_by_rows(right, left), 0)
    key_term = jnp.dot(high, queries, preferred_element_type=jnp.float32) + jnp.dot(
        low, queries, preferred_element_type=jnp.float32
    )
    return per_head(query_term), key_term


def hand_out_kernel(values_ref, factors_ref, *out_refs):
    out_refs[0][...] = values_ref[...]
    start = 0
    for out_ref in out_refs[1:]:
        out_ref[...] = factors_ref[start : start + out_ref.shape[0], :]
        start += out_ref.shape[0]


def gathered_form(n, grad_out, cached, values, query_x, key_x, query_y, key_y):
    x_rows, y_count = grad_out.shape[:2]
    x_count, y_rows = cached.shape[:2]
    term_rows = 2 * (x_rows + y_rows)
    vmem = pl.BlockSpec(memory_space=pltpu.VMEM)
    grad_values, factors = pl.pallas_call(
        functools.partial(gather_kernel, n, x_rows, y_rows),
        out_shape=(
            pltpu.VMEM(values.shape, values.dtype),
            pltpu.VMEM((term_rows, CHANNELS), jnp.float32),
        ),
        in_specs=[pl.BlockSpec(memory_space=pltpu.HBM)] * 7,
        out_specs=(vmem, vmem),
        scratch_shapes=[
            pltpu.VMEM((n, x_rows * y_count, CHANNELS), jnp.bfloat16),
            pltpu.VMEM((y_rows * x_count, CHANNELS), jnp.bfloat16),
            pltpu.VMEM((x_rows * y_count, CHANNELS), jnp.bfloat16),
            pltpu.VMEM(query_x.shape, query_x.dtype),
            pltpu.VMEM(key_x.shape, key_x.dtype),
            pltpu.VMEM(query_y.shape, query_y.dtype),
            pltpu.VMEM(key_y.shape, key_y.dtype),
            pltpu.VMEM((x_count, x_rows * CHANNELS), jnp.float32),
            pltpu.VMEM((x_count * y_count, CHANNELS), jnp.float32),
            pltpu.VMEM((n, term_rows, CHANNELS), jnp.float32),
            pltpu.VMEM((n, term_rows, CHANNELS), jnp.float32),
            pltpu.SemaphoreType.DMA((7,)),
            pltpu.SemaphoreType.DMA((n, n)),
            pltpu.SemaphoreType.DMA((n,)),
            pltpu.SemaphoreType.DMA((n,)),
            pltpu.SemaphoreType.DMA((n,)),
        ],
        compiler_params=pltpu.CompilerParams(
            collective_id=0, has_side_effects=True, vmem_limit_bytes=KERNEL_BYTES
        ),
    )(
        *(
            pltpu.with_memory_space_constraint(array, pltpu.HBM)
            for array in (
                grad_out.reshape(x_rows * y_count, CHANNELS),
                cached.transpose(1, 0, 2).reshape(y_rows * x_count, CHANNELS),
                values.reshape(x_rows * y_count, CHANNELS),
                query_x,
                key_x,
                query_y,
                key_y,
            )
        )
    )
    counts = (x_rows, x_rows, y_rows, y_rows)
    return pl.pallas_call(
        hand_out_kernel,
        out_shape=(jax.ShapeDtypeStruct(values.shape, values.dtype),)
        + tuple(jax.ShapeDtypeStruct((count, CHANNELS), jnp.float32) for count in counts),
        in_specs=[vmem] * 2,
        out_specs=(vmem,) * 5,
        compiler_params=pltpu.CompilerParams(vmem_limit_bytes=KERNEL_BYTES),
    )(grad_values, factors)


GATHERED_BYTES = 1 << 20
KERNEL_BYTES = 16 << 20


def on_device(n, *arrays):
    if n % 2 == 0 and arrays[0].size * arrays[0].dtype.itemsize * n <= GATHERED_BYTES:
        return gathered_form(n, *arrays)
    return exchanged_form(*arrays)


def solution(mesh):
    return jax.shard_map(
        functools.partial(on_device, mesh.shape["slab"]),
        mesh=mesh,
        in_specs=(
            P(("traj", "slab"), None, None),
            P("traj", "slab", None),
            P(("traj", "slab"), None, None),
            P("traj", None),
            P("traj", None),
            P("traj", None),
            P("traj", None),
        ),
        out_specs=(
            P(("traj", "slab"), None, None),
            P(("traj", "slab"), None),
            P(("traj", "slab"), None),
            P(("traj", "slab"), None),
            P(("traj", "slab"), None),
        ),
        check_vma=False,
    )
```

```python
import functools
import math

import jax
import jax.numpy as jnp
from jax import lax
from jax.experimental import pallas as pl
from jax.experimental.pallas import tpu as pltpu
from jax.sharding import PartitionSpec as P

HEADS = 4
HEAD = 32
CHANNELS = HEADS * HEAD


def axis_kernel(queries, key_rows):
    scores = jnp.dot(queries, key_rows.T, preferred_element_type=jnp.float32) / math.sqrt(HEAD)
    return jax.nn.softmax(scores, axis=1)


def local_terms(kernel, coupling, queries, key_rows):
    row_delta = jnp.sum(kernel * coupling, axis=1)
    weighted = kernel * coupling
    grad_query = jnp.dot(
        weighted, key_rows.astype(jnp.float32), precision=lax.Precision.HIGHEST
    ) / math.sqrt(HEAD)
    grad_key = jnp.dot(
        weighted.T, queries.astype(jnp.float32), precision=lax.Precision.HIGHEST
    ) / math.sqrt(HEAD)
    return (grad_query, grad_key, row_delta)


def corrections(own_rows, own_cols, delta_total, queries, key_rows, start, count):
    own_delta = lax.dynamic_slice_in_dim(delta_total, start, count, 0)
    query_fix = (
        own_delta[:, None]
        * jnp.dot(own_rows, key_rows.astype(jnp.float32), precision=lax.Precision.HIGHEST)
        / math.sqrt(HEAD)
    )
    key_fix = jnp.dot(
        own_cols.T,
        delta_total[:, None] * queries.astype(jnp.float32),
        precision=lax.Precision.HIGHEST,
    ) / math.sqrt(HEAD)
    return (query_fix, key_fix)


def exchanged_form(grad_out, cached, values, query_x, key_x, query_y, key_y):
    index = lax.axis_index("slab")
    x_rows = grad_out.shape[0]
    x_count = cached.shape[0]
    y_rows = cached.shape[1]
    x_start = index * x_rows
    y_start = index * y_rows
    grad_columns = lax.all_to_all(grad_out, "slab", split_axis=1, concat_axis=0, tiled=True)
    mixed_heads = []
    query_terms = []
    key_terms = []
    delta_terms = []
    row_slices = []
    col_slices = []
    for head_index in range(HEADS):
        offset = head_index * HEAD
        head_query = query_x[:, offset : offset + HEAD]
        head_key = key_x[:, offset : offset + HEAD]
        kernel = axis_kernel(head_query, head_key)
        grad_rows = grad_columns[:, :, offset : offset + HEAD].reshape(x_count, y_rows * HEAD)
        saved_rows = cached[:, :, offset : offset + HEAD].reshape(x_count, y_rows * HEAD)
        grad_mixed = lax.dot_general(
            kernel.astype(jnp.bfloat16),
            grad_rows,
            (((0,), (0,)), ((), ())),
            preferred_element_type=jnp.float32,
        ).astype(jnp.bfloat16)
        coupling = lax.dot_general(
            grad_rows, saved_rows, (((1,), (1,)), ((), ())), preferred_element_type=jnp.float32
        )
        grad_query, grad_key, row_delta = local_terms(kernel, coupling, head_query, head_key)
        query_terms.append(grad_query)
        key_terms.append(grad_key)
        delta_terms.append(row_delta)
        row_slices.append(lax.dynamic_slice_in_dim(kernel, x_start, x_rows, 0))
        col_slices.append(lax.dynamic_slice_in_dim(kernel, x_start, x_rows, 1))
        mixed_heads.append(grad_mixed.reshape(x_count, y_rows, HEAD))
    mixed_rows = lax.all_to_all(
        jnp.concatenate(mixed_heads, axis=2), "slab", split_axis=0, concat_axis=1, tiled=True
    )
    x_delta_total = lax.psum(jnp.stack(delta_terms), "slab")
    query_x_grad, key_x_grad = (
        lax.psum_scatter(
            jnp.concatenate(query_terms, axis=1), "slab", scatter_dimension=0, tiled=True
        ),
        lax.psum_scatter(
            jnp.concatenate(key_terms, axis=1), "slab", scatter_dimension=0, tiled=True
        ),
    )
    query_fixes = []
    key_fixes = []
    for head_index in range(HEADS):
        offset = head_index * HEAD
        query_fix, key_fix = corrections(
            row_slices[head_index],
            col_slices[head_index],
            x_delta_total[head_index],
            query_x[:, offset : offset + HEAD],
            key_x[:, offset : offset + HEAD],
            x_start,
            x_rows,
        )
        query_fixes.append(query_fix)
        key_fixes.append(key_fix)
    query_x_grad = query_x_grad - jnp.concatenate(query_fixes, axis=1)
    key_x_grad = key_x_grad - jnp.concatenate(key_fixes, axis=1)
    value_heads = []
    query_terms = []
    key_terms = []
    delta_terms = []
    row_slices = []
    col_slices = []
    for head_index in range(HEADS):
        offset = head_index * HEAD
        head_query = query_y[:, offset : offset + HEAD]
        head_key = key_y[:, offset : offset + HEAD]
        kernel = axis_kernel(head_query, head_key)
        mixed_head = mixed_rows[:, :, offset : offset + HEAD]
        value_head = values[:, :, offset : offset + HEAD]
        grad_value = jnp.einsum(
            "jk,xje->xke",
            kernel.astype(jnp.bfloat16),
            mixed_head,
            preferred_element_type=jnp.float32,
        )
        coupling = jnp.einsum(
            "xje,xke->jk", mixed_head, value_head, preferred_element_type=jnp.float32
        )
        grad_query, grad_key, row_delta = local_terms(kernel, coupling, head_query, head_key)
        query_terms.append(grad_query)
        key_terms.append(grad_key)
        delta_terms.append(row_delta)
        row_slices.append(lax.dynamic_slice_in_dim(kernel, y_start, y_rows, 0))
        col_slices.append(lax.dynamic_slice_in_dim(kernel, y_start, y_rows, 1))
        value_heads.append(grad_value.astype(jnp.bfloat16))
    y_delta_total = lax.psum(jnp.stack(delta_terms), "slab")
    query_y_grad, key_y_grad = (
        lax.psum_scatter(
            jnp.concatenate(query_terms, axis=1), "slab", scatter_dimension=0, tiled=True
        ),
        lax.psum_scatter(
            jnp.concatenate(key_terms, axis=1), "slab", scatter_dimension=0, tiled=True
        ),
    )
    query_fixes = []
    key_fixes = []
    for head_index in range(HEADS):
        offset = head_index * HEAD
        query_fix, key_fix = corrections(
            row_slices[head_index],
            col_slices[head_index],
            y_delta_total[head_index],
            query_y[:, offset : offset + HEAD],
            key_y[:, offset : offset + HEAD],
            y_start,
            y_rows,
        )
        query_fixes.append(query_fix)
        key_fixes.append(key_fix)
    query_y_grad = query_y_grad - jnp.concatenate(query_fixes, axis=1)
    key_y_grad = key_y_grad - jnp.concatenate(key_fixes, axis=1)
    grad_values = jnp.concatenate(value_heads, axis=2)
    return (grad_values, query_x_grad, key_x_grad, query_y_grad, key_y_grad)


MESH = pl.DeviceIdType.MESH
ROWS_BY_ROWS = (((1,), (1,)), ((), ()))


def gather_kernel(
    n,
    x_rows,
    y_rows,
    grad_hbm,
    cached_hbm,
    values_hbm,
    query_x_hbm,
    key_x_hbm,
    query_y_hbm,
    key_y_hbm,
    grad_values_ref,
    factors_ref,
    gathered,
    cached_ref,
    values_ref,
    query_x_ref,
    key_x_ref,
    query_y_ref,
    key_y_ref,
    query_x,
    query_y,
    kernel_x,
    kernel_x_turned,
    kernel_y,
    kernel_y_turned,
    cached_lanes,
    values_lanes,
    spread,
    wide,
    outgoing,
    incoming,
    own_sems,
    gather_send,
    gather_recv,
    term_send,
    term_recv,
):
    me = lax.axis_index("slab")
    late = me // (n // 2)
    peers = [lax.rem(me + (2 * late - 1) * step + n, n) for step in range(1, n)]
    x_count, y_count = query_x_ref.shape[0], query_y_ref.shape[0]

    own_grad = pltpu.make_async_copy(grad_hbm, gathered.at[me], own_sems.at[6])
    own_grad.start()
    barrier = pltpu.get_barrier_semaphore()
    for peer in peers:
        pl.semaphore_signal(barrier, inc=1, device_id={"slab": peer}, device_id_type=MESH)
    own_pairs = (
        (query_x_hbm, query_x_ref),
        (key_x_hbm, key_x_ref),
        (query_y_hbm, query_y_ref),
        (key_y_hbm, key_y_ref),
        (cached_hbm, cached_ref),
        (values_hbm, values_ref),
    )
    own = [
        pltpu.make_async_copy(source, target, own_sems.at[place])
        for place, (source, target) in enumerate(own_pairs)
    ]
    for copy in own:
        copy.start()

    def prepare():
        for copy in own:
            copy.wait()
        for queries_ref, keys_ref, heads, kernel, turned in (
            (query_x_ref, key_x_ref, query_x, kernel_x, kernel_x_turned),
            (query_y_ref, key_y_ref, query_y, kernel_y, kernel_y_turned),
        ):
            heads[...] = by_head(queries_ref[...].astype(jnp.float32))
            kernel[...], turned[...] = both_kernels(heads[...], keys_ref[...])
        width = x_rows * CHANNELS
        rows = lax.broadcasted_iota(jnp.int32, (x_count, width), 0)
        lanes = lax.broadcasted_iota(jnp.int32, (x_count, width), 1)
        own_columns = (rows == me * x_rows + lanes // CHANNELS).astype(jnp.bfloat16)
        spread[...] = per_head(
            jnp.dot(
                kernel_x[...].astype(jnp.bfloat16),
                own_columns,
                preferred_element_type=jnp.float32,
            )
        )
        for source, count, target in (
            (cached_ref, x_count, cached_lanes),
            (values_ref, y_count, values_lanes),
        ):
            array = source[...].astype(jnp.float32)
            target[...] = jnp.concatenate(
                [array[r : r + count] for r in range(0, array.shape[0], count)], axis=1
            ).astype(jnp.bfloat16)

    pl.when(late == 0)(prepare)
    own_grad.wait()
    pl.semaphore_wait(barrier, n - 1)
    gathers = []
    for peer in peers:
        copy = pltpu.make_async_remote_copy(
            src_ref=gathered.at[me],
            dst_ref=gathered.at[me],
            send_sem=gather_send.at[peer],
            recv_sem=gather_recv.at[me],
            device_id={"slab": peer},
            device_id_type=MESH,
        )
        copy.start()
        gathers.append(copy)
    pl.when(late == 1)(prepare)

    mixed = [jnp.zeros((y_count, CHANNELS), jnp.float32) for _ in range(x_rows)]
    for slot in [me] + peers[::-1]:
        if slot is not me:
            pltpu.make_async_remote_copy(
                src_ref=gathered.at[me],
                dst_ref=gathered.at[slot],
                send_sem=gather_send.at[slot],
                recv_sem=gather_recv.at[slot],
                device_id={"slab": slot},
                device_id_type=MESH,
            ).wait_recv()
        block = gathered[slot].astype(jnp.float32)
        rows = x_rows * y_count
        wide[pl.ds(pl.multiple_of(slot * rows, 8), rows), :] = block
        for r in range(x_rows):
            row = block[r * y_count : (r + 1) * y_count, :]
            factor = spread[pl.ds(slot * x_rows + r, 1), :]
            for x in range(x_rows):
                mixed[x] += row * factor[:, x * CHANNELS : (x + 1) * CHANNELS]
    grad_columns = jnp.concatenate(
        [
            wide[pl.ds(me * y_rows + y, x_count, stride=y_count), :]
            for y in range(y_rows)
        ],
        axis=1,
    )
    grad_columns = by_head(grad_columns)
    mixed = by_head(jnp.concatenate(mixed, axis=1).astype(jnp.bfloat16).astype(jnp.float32))
    query_x_term, key_x_term = factor_terms(
        kernel_x[...],
        kernel_x_turned[...],
        grad_columns,
        cached_lanes[...],
        query_x[...],
        key_x_ref[...],
    )
    query_y_term, key_y_term = factor_terms(
        kernel_y[...],
        kernel_y_turned[...],
        mixed,
        values_lanes[...],
        query_y[...],
        key_y_ref[...],
    )
    for slot in range(n):
        start = 0
        for term, count in (
            (query_x_term, x_rows),
            (key_x_term, x_rows),
            (query_y_term, y_rows),
            (key_y_term, y_rows),
        ):
            outgoing[slot, start : start + count, :] = term[slot * count : (slot + 1) * count]
            start += count
    terms = []
    for peer in peers:
        copy = pltpu.make_async_remote_copy(
            src_ref=outgoing.at[peer],
            dst_ref=incoming.at[me],
            send_sem=term_send.at[peer],
            recv_sem=term_recv.at[me],
            device_id={"slab": peer},
            device_id_type=MESH,
        )
        copy.start()
        terms.append(copy)

    grad_values = jnp.dot(
        kernel_y_turned[...].astype(jnp.bfloat16), mixed, preferred_element_type=jnp.float32
    )
    for x in range(x_rows):
        grad_values_ref[x] = grad_values[:, x * CHANNELS : (x + 1) * CHANNELS].astype(
            grad_values_ref.dtype
        )

    total = outgoing[me]
    for peer in peers[::-1]:
        pltpu.make_async_remote_copy(
            src_ref=outgoing.at[peer],
            dst_ref=incoming.at[peer],
            send_sem=term_send.at[peer],
            recv_sem=term_recv.at[peer],
            device_id={"slab": peer},
            device_id_type=MESH,
        ).wait_recv()
        total += incoming[peer]
    factors_ref[...] = total * (1.0 / math.sqrt(HEAD))
    for copy in gathers + terms:
        copy.wait_send()


def in_head(head, columns):
    lanes = lax.broadcasted_iota(jnp.int32, (1, CHANNELS), 1)
    mask = (lanes >= head * HEAD) & (lanes < (head + 1) * HEAD)
    return jnp.concatenate([mask] * (columns // CHANNELS), axis=1)


def by_head(array):
    return jnp.concatenate(
        [jnp.where(in_head(head, array.shape[1]), array, 0.0) for head in range(HEADS)], axis=0
    ).astype(jnp.bfloat16)


def per_head(array):
    rows = array.shape[0] // HEADS
    picked = array[:rows]
    for head in range(1, HEADS):
        picked = jnp.where(
            in_head(head, array.shape[1]), array[head * rows : (head + 1) * rows], picked
        )
    return picked


def rows_by_rows(left, right):
    return lax.dot_general(left, right, ROWS_BY_ROWS, preferred_element_type=jnp.float32)


def both_kernels(queries, key_rows):
    kernels = []
    for scores, axis in (
        (rows_by_rows(queries, key_rows), 1),
        (rows_by_rows(key_rows, queries), 0),
    ):
        scores = scores / math.sqrt(HEAD)
        weights = jnp.exp(scores - jnp.max(scores, axis=axis, keepdims=True))
        kernels.append(weights / jnp.sum(weights, axis=axis, keepdims=True))
    return kernels


def weighted_parts(kernel, coupling, axis):
    delta = jnp.sum(kernel * coupling, axis=axis, keepdims=True)
    weighted = kernel * (coupling - delta)
    high = weighted.astype(jnp.bfloat16)
    return high, (weighted - high.astype(jnp.float32)).astype(jnp.bfloat16)


def factor_terms(kernel, kernel_turned, left, right, queries, key_rows):
    high, low = weighted_parts(kernel, rows_by_rows(left, right), 1)
    query_term = jnp.dot(high, key_rows, preferred_element_type=jnp.float32) + jnp.dot(
        low, key_rows, preferred_element_type=jnp.float32
    )
    high, low = weighted_parts(kernel_turned, rows_by_rows(right, left), 0)
    key_term = jnp.dot(high, queries, preferred_element_type=jnp.float32) + jnp.dot(
        low, queries, preferred_element_type=jnp.float32
    )
    return per_head(query_term), key_term


def hand_out_kernel(values_ref, factors_ref, *out_refs):
    out_refs[0][...] = values_ref[...]
    start = 0
    for out_ref in out_refs[1:]:
        out_ref[...] = factors_ref[start : start + out_ref.shape[0], :]
        start += out_ref.shape[0]


def gathered_form(n, grad_out, cached, values, query_x, key_x, query_y, key_y):
    x_rows, y_count = grad_out.shape[:2]
    x_count, y_rows = cached.shape[:2]
    term_rows = 2 * (x_rows + y_rows)
    vmem = pl.BlockSpec(memory_space=pltpu.VMEM)
    grad_values, factors = pl.pallas_call(
        functools.partial(gather_kernel, n, x_rows, y_rows),
        out_shape=(
            pltpu.VMEM(values.shape, values.dtype),
            pltpu.VMEM((term_rows, CHANNELS), jnp.float32),
        ),
        in_specs=[pl.BlockSpec(memory_space=pltpu.HBM)] * 7,
        out_specs=(vmem, vmem),
        scratch_shapes=[
            pltpu.VMEM((n, x_rows * y_count, CHANNELS), jnp.bfloat16),
            pltpu.VMEM((y_rows * x_count, CHANNELS), jnp.bfloat16),
            pltpu.VMEM((x_rows * y_count, CHANNELS), jnp.bfloat16),
            pltpu.VMEM(query_x.shape, query_x.dtype),
            pltpu.VMEM(key_x.shape, key_x.dtype),
            pltpu.VMEM(query_y.shape, query_y.dtype),
            pltpu.VMEM(key_y.shape, key_y.dtype),
            pltpu.VMEM((HEADS * x_count, CHANNELS), jnp.bfloat16),
            pltpu.VMEM((HEADS * y_count, CHANNELS), jnp.bfloat16),
            pltpu.VMEM((HEADS * x_count, x_count), jnp.float32),
            pltpu.VMEM((x_count, HEADS * x_count), jnp.float32),
            pltpu.VMEM((HEADS * y_count, y_count), jnp.float32),
            pltpu.VMEM((y_count, HEADS * y_count), jnp.float32),
            pltpu.VMEM((x_count, y_rows * CHANNELS), jnp.bfloat16),
            pltpu.VMEM((y_count, x_rows * CHANNELS), jnp.bfloat16),
            pltpu.VMEM((x_count, x_rows * CHANNELS), jnp.float32),
            pltpu.VMEM((x_count * y_count, CHANNELS), jnp.float32),
            pltpu.VMEM((n, term_rows, CHANNELS), jnp.float32),
            pltpu.VMEM((n, term_rows, CHANNELS), jnp.float32),
            pltpu.SemaphoreType.DMA((7,)),
            pltpu.SemaphoreType.DMA((n,)),
            pltpu.SemaphoreType.DMA((n,)),
            pltpu.SemaphoreType.DMA((n,)),
            pltpu.SemaphoreType.DMA((n,)),
        ],
        compiler_params=pltpu.CompilerParams(
            collective_id=0, has_side_effects=True, vmem_limit_bytes=KERNEL_BYTES
        ),
    )(
        *(
            pltpu.with_memory_space_constraint(array, pltpu.HBM)
            for array in (
                grad_out.reshape(x_rows * y_count, CHANNELS),
                cached.transpose(1, 0, 2).reshape(y_rows * x_count, CHANNELS),
                values.reshape(x_rows * y_count, CHANNELS),
                query_x,
                key_x,
                query_y,
                key_y,
            )
        )
    )
    counts = (x_rows, x_rows, y_rows, y_rows)
    return pl.pallas_call(
        hand_out_kernel,
        out_shape=(jax.ShapeDtypeStruct(values.shape, values.dtype),)
        + tuple(jax.ShapeDtypeStruct((count, CHANNELS), jnp.float32) for count in counts),
        in_specs=[vmem] * 2,
        out_specs=(vmem,) * 5,
        compiler_params=pltpu.CompilerParams(vmem_limit_bytes=KERNEL_BYTES),
    )(grad_values, factors)


GATHERED_BYTES = 1 << 20
KERNEL_BYTES = 16 << 20


def on_device(n, *arrays):
    if n % 2 == 0 and arrays[0].size * arrays[0].dtype.itemsize * n <= GATHERED_BYTES:
        return gathered_form(n, *arrays)
    return exchanged_form(*arrays)


def solution(mesh):
    return jax.shard_map(
        functools.partial(on_device, mesh.shape["slab"]),
        mesh=mesh,
        in_specs=(
            P(("traj", "slab"), None, None),
            P("traj", "slab", None),
            P(("traj", "slab"), None, None),
            P("traj", None),
            P("traj", None),
            P("traj", None),
            P("traj", None),
        ),
        out_specs=(
            P(("traj", "slab"), None, None),
            P(("traj", "slab"), None),
            P(("traj", "slab"), None),
            P(("traj", "slab"), None),
            P(("traj", "slab"), None),
        ),
        check_vma=False,
    )
```

```python
import functools
import math

import jax
import jax.numpy as jnp
from jax import lax
from jax.experimental import pallas as pl
from jax.experimental.pallas import tpu as pltpu
from jax.sharding import PartitionSpec as P

HEADS = 4
HEAD = 32
CHANNELS = HEADS * HEAD


def axis_kernel(queries, key_rows):
    scores = jnp.dot(queries, key_rows.T, preferred_element_type=jnp.float32) / math.sqrt(HEAD)
    return jax.nn.softmax(scores, axis=1)


def local_terms(kernel, coupling, queries, key_rows):
    row_delta = jnp.sum(kernel * coupling, axis=1)
    weighted = kernel * coupling
    grad_query = jnp.dot(
        weighted, key_rows.astype(jnp.float32), precision=lax.Precision.HIGHEST
    ) / math.sqrt(HEAD)
    grad_key = jnp.dot(
        weighted.T, queries.astype(jnp.float32), precision=lax.Precision.HIGHEST
    ) / math.sqrt(HEAD)
    return (grad_query, grad_key, row_delta)


def corrections(own_rows, own_cols, delta_total, queries, key_rows, start, count):
    own_delta = lax.dynamic_slice_in_dim(delta_total, start, count, 0)
    query_fix = (
        own_delta[:, None]
        * jnp.dot(own_rows, key_rows.astype(jnp.float32), precision=lax.Precision.HIGHEST)
        / math.sqrt(HEAD)
    )
    key_fix = jnp.dot(
        own_cols.T,
        delta_total[:, None] * queries.astype(jnp.float32),
        precision=lax.Precision.HIGHEST,
    ) / math.sqrt(HEAD)
    return (query_fix, key_fix)


def exchanged_form(grad_out, cached, values, query_x, key_x, query_y, key_y):
    index = lax.axis_index("slab")
    x_rows = grad_out.shape[0]
    x_count = cached.shape[0]
    y_rows = cached.shape[1]
    x_start = index * x_rows
    y_start = index * y_rows
    grad_columns = lax.all_to_all(grad_out, "slab", split_axis=1, concat_axis=0, tiled=True)
    mixed_heads = []
    query_terms = []
    key_terms = []
    delta_terms = []
    row_slices = []
    col_slices = []
    for head_index in range(HEADS):
        offset = head_index * HEAD
        head_query = query_x[:, offset : offset + HEAD]
        head_key = key_x[:, offset : offset + HEAD]
        kernel = axis_kernel(head_query, head_key)
        grad_rows = grad_columns[:, :, offset : offset + HEAD].reshape(x_count, y_rows * HEAD)
        saved_rows = cached[:, :, offset : offset + HEAD].reshape(x_count, y_rows * HEAD)
        grad_mixed = lax.dot_general(
            kernel.astype(jnp.bfloat16),
            grad_rows,
            (((0,), (0,)), ((), ())),
            preferred_element_type=jnp.float32,
        ).astype(jnp.bfloat16)
        coupling = lax.dot_general(
            grad_rows, saved_rows, (((1,), (1,)), ((), ())), preferred_element_type=jnp.float32
        )
        grad_query, grad_key, row_delta = local_terms(kernel, coupling, head_query, head_key)
        query_terms.append(grad_query)
        key_terms.append(grad_key)
        delta_terms.append(row_delta)
        row_slices.append(lax.dynamic_slice_in_dim(kernel, x_start, x_rows, 0))
        col_slices.append(lax.dynamic_slice_in_dim(kernel, x_start, x_rows, 1))
        mixed_heads.append(grad_mixed.reshape(x_count, y_rows, HEAD))
    mixed_rows = lax.all_to_all(
        jnp.concatenate(mixed_heads, axis=2), "slab", split_axis=0, concat_axis=1, tiled=True
    )
    x_delta_total = lax.psum(jnp.stack(delta_terms), "slab")
    query_x_grad, key_x_grad = (
        lax.psum_scatter(
            jnp.concatenate(query_terms, axis=1), "slab", scatter_dimension=0, tiled=True
        ),
        lax.psum_scatter(
            jnp.concatenate(key_terms, axis=1), "slab", scatter_dimension=0, tiled=True
        ),
    )
    query_fixes = []
    key_fixes = []
    for head_index in range(HEADS):
        offset = head_index * HEAD
        query_fix, key_fix = corrections(
            row_slices[head_index],
            col_slices[head_index],
            x_delta_total[head_index],
            query_x[:, offset : offset + HEAD],
            key_x[:, offset : offset + HEAD],
            x_start,
            x_rows,
        )
        query_fixes.append(query_fix)
        key_fixes.append(key_fix)
    query_x_grad = query_x_grad - jnp.concatenate(query_fixes, axis=1)
    key_x_grad = key_x_grad - jnp.concatenate(key_fixes, axis=1)
    value_heads = []
    query_terms = []
    key_terms = []
    delta_terms = []
    row_slices = []
    col_slices = []
    for head_index in range(HEADS):
        offset = head_index * HEAD
        head_query = query_y[:, offset : offset + HEAD]
        head_key = key_y[:, offset : offset + HEAD]
        kernel = axis_kernel(head_query, head_key)
        mixed_head = mixed_rows[:, :, offset : offset + HEAD]
        value_head = values[:, :, offset : offset + HEAD]
        grad_value = jnp.einsum(
            "jk,xje->xke",
            kernel.astype(jnp.bfloat16),
            mixed_head,
            preferred_element_type=jnp.float32,
        )
        coupling = jnp.einsum(
            "xje,xke->jk", mixed_head, value_head, preferred_element_type=jnp.float32
        )
        grad_query, grad_key, row_delta = local_terms(kernel, coupling, head_query, head_key)
        query_terms.append(grad_query)
        key_terms.append(grad_key)
        delta_terms.append(row_delta)
        row_slices.append(lax.dynamic_slice_in_dim(kernel, y_start, y_rows, 0))
        col_slices.append(lax.dynamic_slice_in_dim(kernel, y_start, y_rows, 1))
        value_heads.append(grad_value.astype(jnp.bfloat16))
    y_delta_total = lax.psum(jnp.stack(delta_terms), "slab")
    query_y_grad, key_y_grad = (
        lax.psum_scatter(
            jnp.concatenate(query_terms, axis=1), "slab", scatter_dimension=0, tiled=True
        ),
        lax.psum_scatter(
            jnp.concatenate(key_terms, axis=1), "slab", scatter_dimension=0, tiled=True
        ),
    )
    query_fixes = []
    key_fixes = []
    for head_index in range(HEADS):
        offset = head_index * HEAD
        query_fix, key_fix = corrections(
            row_slices[head_index],
            col_slices[head_index],
            y_delta_total[head_index],
            query_y[:, offset : offset + HEAD],
            key_y[:, offset : offset + HEAD],
            y_start,
            y_rows,
        )
        query_fixes.append(query_fix)
        key_fixes.append(key_fix)
    query_y_grad = query_y_grad - jnp.concatenate(query_fixes, axis=1)
    key_y_grad = key_y_grad - jnp.concatenate(key_fixes, axis=1)
    grad_values = jnp.concatenate(value_heads, axis=2)
    return (grad_values, query_x_grad, key_x_grad, query_y_grad, key_y_grad)


MESH = pl.DeviceIdType.MESH
ROWS_BY_ROWS = (((1,), (1,)), ((), ()))


def gather_kernel(
    n,
    x_rows,
    y_rows,
    grad_hbm,
    cached_hbm,
    values_hbm,
    query_x_hbm,
    key_x_hbm,
    query_y_hbm,
    key_y_hbm,
    grad_values_ref,
    factors_ref,
    gathered,
    cached_ref,
    values_ref,
    query_x_ref,
    key_x_ref,
    query_y_ref,
    key_y_ref,
    query_x,
    query_y,
    kernel_x,
    kernel_x_turned,
    kernel_y,
    kernel_y_turned,
    cached_lanes,
    values_lanes,
    spread,
    wide,
    packing,
    outgoing,
    incoming,
    own_sems,
    gather_send,
    gather_recv,
    term_send,
    term_recv,
):
    me = lax.axis_index("slab")
    late = me // (n // 2)
    peers = [lax.rem(me + (2 * late - 1) * step + n, n) for step in range(1, n)]
    x_count, y_count = query_x_ref.shape[0], query_y_ref.shape[0]
    term_rows = factors_ref.shape[0]

    own_grad = pltpu.make_async_copy(grad_hbm, gathered.at[me], own_sems.at[6])
    own_grad.start()
    barrier = pltpu.get_barrier_semaphore()
    for peer in peers:
        pl.semaphore_signal(barrier, inc=1, device_id={"slab": peer}, device_id_type=MESH)
    own_pairs = (
        (query_x_hbm, query_x_ref),
        (key_x_hbm, key_x_ref),
        (query_y_hbm, query_y_ref),
        (key_y_hbm, key_y_ref),
        (cached_hbm, cached_ref),
        (values_hbm, values_ref),
    )
    own = [
        pltpu.make_async_copy(source, target, own_sems.at[place])
        for place, (source, target) in enumerate(own_pairs)
    ]
    for copy in own:
        copy.start()

    def prepare():
        for copy in own:
            copy.wait()
        for queries_ref, keys_ref, heads, kernel, turned in (
            (query_x_ref, key_x_ref, query_x, kernel_x, kernel_x_turned),
            (query_y_ref, key_y_ref, query_y, kernel_y, kernel_y_turned),
        ):
            heads[...] = by_head(queries_ref[...].astype(jnp.float32))
            kernel[...], turned[...] = both_kernels(heads[...], keys_ref[...])
        width = x_rows * CHANNELS
        rows = lax.broadcasted_iota(jnp.int32, (x_count, width), 0)
        lanes = lax.broadcasted_iota(jnp.int32, (x_count, width), 1)
        own_columns = (rows == me * x_rows + lanes // CHANNELS).astype(jnp.bfloat16)
        spread[...] = per_head(
            jnp.dot(
                kernel_x[...].astype(jnp.bfloat16),
                own_columns,
                preferred_element_type=jnp.float32,
            )
        )
        for source, count, target in (
            (cached_ref, x_count, cached_lanes),
            (values_ref, y_count, values_lanes),
        ):
            array = source[...].astype(jnp.float32)
            target[...] = jnp.concatenate(
                [array[r : r + count] for r in range(0, array.shape[0], count)], axis=1
            ).astype(jnp.bfloat16)

    def gathers(source):
        return [
            pltpu.make_async_remote_copy(
                src_ref=source,
                dst_ref=gathered.at[me],
                send_sem=gather_send.at[peer],
                recv_sem=gather_recv.at[me],
                device_id={"slab": peer},
                device_id_type=MESH,
            )
            for peer in peers
        ]

    @pl.when(late == 0)
    def _():
        prepare()
        own_grad.wait()
        pl.semaphore_wait(barrier, n - 1)
        for copy in gathers(gathered.at[me]):
            copy.start()

    @pl.when(late == 1)
    def _():
        pl.semaphore_wait(barrier, n - 1)
        for copy in gathers(grad_hbm):
            copy.start()
        prepare()
        own_grad.wait()

    mixed = [jnp.zeros((y_count, CHANNELS), jnp.float32) for _ in range(x_rows)]
    for slot in [me] + peers[::-1]:
        if slot is not me:
            pltpu.make_async_remote_copy(
                src_ref=gathered.at[me],
                dst_ref=gathered.at[slot],
                send_sem=gather_send.at[slot],
                recv_sem=gather_recv.at[slot],
                device_id={"slab": slot},
                device_id_type=MESH,
            ).wait_recv()
        block = gathered[slot].astype(jnp.float32)
        rows = x_rows * y_count
        wide[pl.ds(pl.multiple_of(slot * rows, 8), rows), :] = block
        for r in range(x_rows):
            row = block[r * y_count : (r + 1) * y_count, :]
            factor = spread[pl.ds(slot * x_rows + r, 1), :]
            for x in range(x_rows):
                mixed[x] += row * factor[:, x * CHANNELS : (x + 1) * CHANNELS]
    grad_columns = jnp.concatenate(
        [
            wide[pl.ds(me * y_rows + y, x_count, stride=y_count), :]
            for y in range(y_rows)
        ],
        axis=1,
    )
    grad_columns = by_head(grad_columns)
    mixed = by_head(jnp.concatenate(mixed, axis=1).astype(jnp.bfloat16).astype(jnp.float32))
    query_x_term, key_x_term = factor_terms(
        kernel_x[...],
        kernel_x_turned[...],
        grad_columns,
        cached_lanes[...],
        query_x[...],
        key_x_ref[...],
    )
    query_y_term, key_y_term = factor_terms(
        kernel_y[...],
        kernel_y_turned[...],
        mixed,
        values_lanes[...],
        query_y[...],
        key_y_ref[...],
    )
    first = 0
    for term, count in (
        (query_x_term, x_rows),
        (key_x_term, x_rows),
        (query_y_term, y_rows),
        (key_y_term, y_rows),
    ):
        packing[pl.ds(n * first, n * count), :] = term
        for r in range(count):
            outgoing[pl.ds(first + r, n, stride=term_rows), :] = packing[
                pl.ds(n * first + r, n, stride=count), :
            ]
        first += count
    def message(peer):
        return pl.ds(pl.multiple_of(peer * term_rows, 8), term_rows)

    terms = []
    for peer in peers:
        copy = pltpu.make_async_remote_copy(
            src_ref=outgoing.at[message(peer)],
            dst_ref=incoming.at[me],
            send_sem=term_send.at[peer],
            recv_sem=term_recv.at[me],
            device_id={"slab": peer},
            device_id_type=MESH,
        )
        copy.start()
        terms.append(copy)

    grad_values = jnp.dot(
        kernel_y_turned[...].astype(jnp.bfloat16), mixed, preferred_element_type=jnp.float32
    )
    for x in range(x_rows):
        grad_values_ref[x] = grad_values[:, x * CHANNELS : (x + 1) * CHANNELS].astype(
            grad_values_ref.dtype
        )

    for copy in gathers(gathered.at[me]) + terms:
        copy.wait_send()
    total = outgoing[message(me), :]
    for peer in peers[::-1]:
        pltpu.make_async_remote_copy(
            src_ref=outgoing.at[message(peer)],
            dst_ref=incoming.at[peer],
            send_sem=term_send.at[peer],
            recv_sem=term_recv.at[peer],
            device_id={"slab": peer},
            device_id_type=MESH,
        ).wait_recv()
        total += incoming[peer]
    factors_ref[...] = total * (1.0 / math.sqrt(HEAD))


def in_head(head, columns):
    lanes = lax.broadcasted_iota(jnp.int32, (1, CHANNELS), 1)
    mask = (lanes >= head * HEAD) & (lanes < (head + 1) * HEAD)
    return jnp.concatenate([mask] * (columns // CHANNELS), axis=1)


def by_head(array):
    return jnp.concatenate(
        [jnp.where(in_head(head, array.shape[1]), array, 0.0) for head in range(HEADS)], axis=0
    ).astype(jnp.bfloat16)


def per_head(array):
    rows = array.shape[0] // HEADS
    picked = array[:rows]
    for head in range(1, HEADS):
        picked = jnp.where(
            in_head(head, array.shape[1]), array[head * rows : (head + 1) * rows], picked
        )
    return picked


def rows_by_rows(left, right):
    return lax.dot_general(left, right, ROWS_BY_ROWS, preferred_element_type=jnp.float32)


def both_kernels(queries, key_rows):
    kernels = []
    for scores, axis in (
        (rows_by_rows(queries, key_rows), 1),
        (rows_by_rows(key_rows, queries), 0),
    ):
        scores = scores / math.sqrt(HEAD)
        weights = jnp.exp(scores - jnp.max(scores, axis=axis, keepdims=True))
        kernels.append(weights / jnp.sum(weights, axis=axis, keepdims=True))
    return kernels


def weighted_parts(kernel, coupling, axis):
    delta = jnp.sum(kernel * coupling, axis=axis, keepdims=True)
    weighted = kernel * (coupling - delta)
    high = weighted.astype(jnp.bfloat16)
    return high, (weighted - high.astype(jnp.float32)).astype(jnp.bfloat16)


def factor_terms(kernel, kernel_turned, left, right, queries, key_rows):
    high, low = weighted_parts(kernel, rows_by_rows(left, right), 1)
    query_term = jnp.dot(high, key_rows, preferred_element_type=jnp.float32) + jnp.dot(
        low, key_rows, preferred_element_type=jnp.float32
    )
    high, low = weighted_parts(kernel_turned, rows_by_rows(right, left), 0)
    key_term = jnp.dot(high, queries, preferred_element_type=jnp.float32) + jnp.dot(
        low, queries, preferred_element_type=jnp.float32
    )
    return per_head(query_term), key_term


def hand_out_kernel(values_ref, factors_ref, *out_refs):
    out_refs[0][...] = values_ref[...]
    start = 0
    for out_ref in out_refs[1:]:
        out_ref[...] = factors_ref[start : start + out_ref.shape[0], :]
        start += out_ref.shape[0]


def gathered_form(n, grad_out, cached, values, query_x, key_x, query_y, key_y):
    x_rows, y_count = grad_out.shape[:2]
    x_count, y_rows = cached.shape[:2]
    term_rows = -(-2 * (x_rows + y_rows) // 8) * 8
    vmem = pl.BlockSpec(memory_space=pltpu.VMEM)
    grad_values, factors = pl.pallas_call(
        functools.partial(gather_kernel, n, x_rows, y_rows),
        out_shape=(
            pltpu.VMEM(values.shape, values.dtype),
            pltpu.VMEM((term_rows, CHANNELS), jnp.float32),
        ),
        in_specs=[pl.BlockSpec(memory_space=pltpu.HBM)] * 7,
        out_specs=(vmem, vmem),
        scratch_shapes=[
            pltpu.VMEM((n, x_rows * y_count, CHANNELS), jnp.bfloat16),
            pltpu.VMEM((y_rows * x_count, CHANNELS), jnp.bfloat16),
            pltpu.VMEM((x_rows * y_count, CHANNELS), jnp.bfloat16),
            pltpu.VMEM(query_x.shape, query_x.dtype),
            pltpu.VMEM(key_x.shape, key_x.dtype),
            pltpu.VMEM(query_y.shape, query_y.dtype),
            pltpu.VMEM(key_y.shape, key_y.dtype),
            pltpu.VMEM((HEADS * x_count, CHANNELS), jnp.bfloat16),
            pltpu.VMEM((HEADS * y_count, CHANNELS), jnp.bfloat16),
            pltpu.VMEM((HEADS * x_count, x_count), jnp.float32),
            pltpu.VMEM((x_count, HEADS * x_count), jnp.float32),
            pltpu.VMEM((HEADS * y_count, y_count), jnp.float32),
            pltpu.VMEM((y_count, HEADS * y_count), jnp.float32),
            pltpu.VMEM((x_count, y_rows * CHANNELS), jnp.bfloat16),
            pltpu.VMEM((y_count, x_rows * CHANNELS), jnp.bfloat16),
            pltpu.VMEM((x_count, x_rows * CHANNELS), jnp.float32),
            pltpu.VMEM(((x_count + 1) * y_count, CHANNELS), jnp.float32),
            pltpu.VMEM((2 * (x_count + y_count) + 8, CHANNELS), jnp.float32),
            pltpu.VMEM(((n + 1) * term_rows, CHANNELS), jnp.float32),
            pltpu.VMEM((n, term_rows, CHANNELS), jnp.float32),
            pltpu.SemaphoreType.DMA((7,)),
            pltpu.SemaphoreType.DMA((n,)),
            pltpu.SemaphoreType.DMA((n,)),
            pltpu.SemaphoreType.DMA((n,)),
            pltpu.SemaphoreType.DMA((n,)),
        ],
        compiler_params=pltpu.CompilerParams(
            collective_id=0, has_side_effects=True, vmem_limit_bytes=KERNEL_BYTES
        ),
    )(
        *(
            pltpu.with_memory_space_constraint(array, pltpu.HBM)
            for array in (
                grad_out.reshape(x_rows * y_count, CHANNELS),
                cached.transpose(1, 0, 2).reshape(y_rows * x_count, CHANNELS),
                values.reshape(x_rows * y_count, CHANNELS),
                query_x,
                key_x,
                query_y,
                key_y,
            )
        )
    )
    counts = (x_rows, x_rows, y_rows, y_rows)
    return pl.pallas_call(
        hand_out_kernel,
        out_shape=(jax.ShapeDtypeStruct(values.shape, values.dtype),)
        + tuple(jax.ShapeDtypeStruct((count, CHANNELS), jnp.float32) for count in counts),
        in_specs=[vmem] * 2,
        out_specs=(vmem,) * 5,
        compiler_params=pltpu.CompilerParams(vmem_limit_bytes=KERNEL_BYTES),
    )(grad_values, factors)


GATHERED_BYTES = 1 << 20
KERNEL_BYTES = 16 << 20


def on_device(n, *arrays):
    if n % 2 == 0 and arrays[0].size * arrays[0].dtype.itemsize * n <= GATHERED_BYTES:
        return gathered_form(n, *arrays)
    return exchanged_form(*arrays)


def solution(mesh):
    return jax.shard_map(
        functools.partial(on_device, mesh.shape["slab"]),
        mesh=mesh,
        in_specs=(
            P(("traj", "slab"), None, None),
            P("traj", "slab", None),
            P(("traj", "slab"), None, None),
            P("traj", None),
            P("traj", None),
            P("traj", None),
            P("traj", None),
        ),
        out_specs=(
            P(("traj", "slab"), None, None),
            P(("traj", "slab"), None),
            P(("traj", "slab"), None),
            P(("traj", "slab"), None),
            P(("traj", "slab"), None),
        ),
        check_vma=False,
    )
```

```python
import functools
import math

import jax
import jax.numpy as jnp
from jax import lax
from jax.experimental import pallas as pl
from jax.experimental.pallas import tpu as pltpu
from jax.sharding import PartitionSpec as P

HEADS = 4
HEAD = 32
CHANNELS = HEADS * HEAD


def axis_kernel(queries, key_rows):
    scores = jnp.dot(queries, key_rows.T, preferred_element_type=jnp.float32) / math.sqrt(HEAD)
    return jax.nn.softmax(scores, axis=1)


def local_terms(kernel, coupling, queries, key_rows):
    row_delta = jnp.sum(kernel * coupling, axis=1)
    weighted = kernel * coupling
    grad_query = jnp.dot(
        weighted, key_rows.astype(jnp.float32), precision=lax.Precision.HIGHEST
    ) / math.sqrt(HEAD)
    grad_key = jnp.dot(
        weighted.T, queries.astype(jnp.float32), precision=lax.Precision.HIGHEST
    ) / math.sqrt(HEAD)
    return (grad_query, grad_key, row_delta)


def corrections(own_rows, own_cols, delta_total, queries, key_rows, start, count):
    own_delta = lax.dynamic_slice_in_dim(delta_total, start, count, 0)
    query_fix = (
        own_delta[:, None]
        * jnp.dot(own_rows, key_rows.astype(jnp.float32), precision=lax.Precision.HIGHEST)
        / math.sqrt(HEAD)
    )
    key_fix = jnp.dot(
        own_cols.T,
        delta_total[:, None] * queries.astype(jnp.float32),
        precision=lax.Precision.HIGHEST,
    ) / math.sqrt(HEAD)
    return (query_fix, key_fix)


def exchanged_form(grad_out, cached, values, query_x, key_x, query_y, key_y):
    index = lax.axis_index("slab")
    x_rows = grad_out.shape[0]
    x_count = cached.shape[0]
    y_rows = cached.shape[1]
    x_start = index * x_rows
    y_start = index * y_rows
    grad_columns = lax.all_to_all(grad_out, "slab", split_axis=1, concat_axis=0, tiled=True)
    mixed_heads = []
    query_terms = []
    key_terms = []
    delta_terms = []
    row_slices = []
    col_slices = []
    for head_index in range(HEADS):
        offset = head_index * HEAD
        head_query = query_x[:, offset : offset + HEAD]
        head_key = key_x[:, offset : offset + HEAD]
        kernel = axis_kernel(head_query, head_key)
        grad_rows = grad_columns[:, :, offset : offset + HEAD].reshape(x_count, y_rows * HEAD)
        saved_rows = cached[:, :, offset : offset + HEAD].reshape(x_count, y_rows * HEAD)
        grad_mixed = lax.dot_general(
            kernel.astype(jnp.bfloat16),
            grad_rows,
            (((0,), (0,)), ((), ())),
            preferred_element_type=jnp.float32,
        ).astype(jnp.bfloat16)
        coupling = lax.dot_general(
            grad_rows, saved_rows, (((1,), (1,)), ((), ())), preferred_element_type=jnp.float32
        )
        grad_query, grad_key, row_delta = local_terms(kernel, coupling, head_query, head_key)
        query_terms.append(grad_query)
        key_terms.append(grad_key)
        delta_terms.append(row_delta)
        row_slices.append(lax.dynamic_slice_in_dim(kernel, x_start, x_rows, 0))
        col_slices.append(lax.dynamic_slice_in_dim(kernel, x_start, x_rows, 1))
        mixed_heads.append(grad_mixed.reshape(x_count, y_rows, HEAD))
    mixed_rows = lax.all_to_all(
        jnp.concatenate(mixed_heads, axis=2), "slab", split_axis=0, concat_axis=1, tiled=True
    )
    x_delta_total = lax.psum(jnp.stack(delta_terms), "slab")
    query_x_grad, key_x_grad = (
        lax.psum_scatter(
            jnp.concatenate(query_terms, axis=1), "slab", scatter_dimension=0, tiled=True
        ),
        lax.psum_scatter(
            jnp.concatenate(key_terms, axis=1), "slab", scatter_dimension=0, tiled=True
        ),
    )
    query_fixes = []
    key_fixes = []
    for head_index in range(HEADS):
        offset = head_index * HEAD
        query_fix, key_fix = corrections(
            row_slices[head_index],
            col_slices[head_index],
            x_delta_total[head_index],
            query_x[:, offset : offset + HEAD],
            key_x[:, offset : offset + HEAD],
            x_start,
            x_rows,
        )
        query_fixes.append(query_fix)
        key_fixes.append(key_fix)
    query_x_grad = query_x_grad - jnp.concatenate(query_fixes, axis=1)
    key_x_grad = key_x_grad - jnp.concatenate(key_fixes, axis=1)
    value_heads = []
    query_terms = []
    key_terms = []
    delta_terms = []
    row_slices = []
    col_slices = []
    for head_index in range(HEADS):
        offset = head_index * HEAD
        head_query = query_y[:, offset : offset + HEAD]
        head_key = key_y[:, offset : offset + HEAD]
        kernel = axis_kernel(head_query, head_key)
        mixed_head = mixed_rows[:, :, offset : offset + HEAD]
        value_head = values[:, :, offset : offset + HEAD]
        grad_value = jnp.einsum(
            "jk,xje->xke",
            kernel.astype(jnp.bfloat16),
            mixed_head,
            preferred_element_type=jnp.float32,
        )
        coupling = jnp.einsum(
            "xje,xke->jk", mixed_head, value_head, preferred_element_type=jnp.float32
        )
        grad_query, grad_key, row_delta = local_terms(kernel, coupling, head_query, head_key)
        query_terms.append(grad_query)
        key_terms.append(grad_key)
        delta_terms.append(row_delta)
        row_slices.append(lax.dynamic_slice_in_dim(kernel, y_start, y_rows, 0))
        col_slices.append(lax.dynamic_slice_in_dim(kernel, y_start, y_rows, 1))
        value_heads.append(grad_value.astype(jnp.bfloat16))
    y_delta_total = lax.psum(jnp.stack(delta_terms), "slab")
    query_y_grad, key_y_grad = (
        lax.psum_scatter(
            jnp.concatenate(query_terms, axis=1), "slab", scatter_dimension=0, tiled=True
        ),
        lax.psum_scatter(
            jnp.concatenate(key_terms, axis=1), "slab", scatter_dimension=0, tiled=True
        ),
    )
    query_fixes = []
    key_fixes = []
    for head_index in range(HEADS):
        offset = head_index * HEAD
        query_fix, key_fix = corrections(
            row_slices[head_index],
            col_slices[head_index],
            y_delta_total[head_index],
            query_y[:, offset : offset + HEAD],
            key_y[:, offset : offset + HEAD],
            y_start,
            y_rows,
        )
        query_fixes.append(query_fix)
        key_fixes.append(key_fix)
    query_y_grad = query_y_grad - jnp.concatenate(query_fixes, axis=1)
    key_y_grad = key_y_grad - jnp.concatenate(key_fixes, axis=1)
    grad_values = jnp.concatenate(value_heads, axis=2)
    return (grad_values, query_x_grad, key_x_grad, query_y_grad, key_y_grad)


MESH = pl.DeviceIdType.MESH
ROWS_BY_ROWS = (((1,), (1,)), ((), ()))


def gather_kernel(
    n,
    x_rows,
    y_rows,
    grad_hbm,
    cached_hbm,
    values_hbm,
    query_x_hbm,
    key_x_hbm,
    query_y_hbm,
    key_y_hbm,
    grad_values_ref,
    factors_ref,
    gathered,
    cached_ref,
    values_ref,
    query_x_ref,
    key_x_ref,
    query_y_ref,
    key_y_ref,
    query_x,
    query_y,
    kernel_x,
    kernel_x_turned,
    kernel_y,
    kernel_y_turned,
    cached_lanes,
    values_lanes,
    spread,
    wide,
    packing,
    outgoing,
    incoming,
    own_sems,
    gather_send,
    gather_recv,
    term_send,
    term_recv,
):
    me = lax.axis_index("slab")
    late = me // (n // 2)
    peers = [lax.rem(me + (2 * late - 1) * step + n, n) for step in range(1, n)]
    mate = me + 1 - 2 * lax.rem(me, 2)
    far = [lax.rem(me + (2 * late - 1) * step + n, n) for step in range(2, n, 2)]
    handed = [lax.rem(mate + step, n) for step in range(2, n, 2)]
    x_count, y_count = query_x_ref.shape[0], query_y_ref.shape[0]

    own_grad = pltpu.make_async_copy(grad_hbm, gathered.at[me], own_sems.at[6])
    own_grad.start()
    barrier = pltpu.get_barrier_semaphore()
    for peer in peers:
        pl.semaphore_signal(barrier, inc=1, device_id={"slab": peer}, device_id_type=MESH)
    own_pairs = (
        (query_x_hbm, query_x_ref),
        (key_x_hbm, key_x_ref),
        (query_y_hbm, query_y_ref),
        (key_y_hbm, key_y_ref),
        (cached_hbm, cached_ref),
        (values_hbm, values_ref),
    )
    own = [
        pltpu.make_async_copy(source, target, own_sems.at[place])
        for place, (source, target) in enumerate(own_pairs)
    ]
    for copy in own:
        copy.start()

    def prepare():
        for copy in own:
            copy.wait()
        for queries_ref, keys_ref, heads, kernel, turned in (
            (query_x_ref, key_x_ref, query_x, kernel_x, kernel_x_turned),
            (query_y_ref, key_y_ref, query_y, kernel_y, kernel_y_turned),
        ):
            heads[...] = by_head(queries_ref[...].astype(jnp.float32))
            kernel[...], turned[...] = both_kernels(heads[...], keys_ref[...])
        width = x_rows * CHANNELS
        rows = lax.broadcasted_iota(jnp.int32, (x_count, width), 0)
        lanes = lax.broadcasted_iota(jnp.int32, (x_count, width), 1)
        own_columns = (rows == me * x_rows + lanes // CHANNELS).astype(jnp.bfloat16)
        spread[...] = per_head(
            jnp.dot(
                kernel_x[...].astype(jnp.bfloat16),
                own_columns,
                preferred_element_type=jnp.float32,
            )
        )
        for source, count, target in (
            (cached_ref, x_count, cached_lanes),
            (values_ref, y_count, values_lanes),
        ):
            array = source[...].astype(jnp.float32)
            target[...] = jnp.concatenate(
                [array[r : r + count] for r in range(0, array.shape[0], count)], axis=1
            ).astype(jnp.bfloat16)

    def block_copy(source, block, target):
        return pltpu.make_async_remote_copy(
            src_ref=source,
            dst_ref=gathered.at[block],
            send_sem=gather_send.at[target, block],
            recv_sem=gather_recv.at[block],
            device_id={"slab": target},
            device_id_type=MESH,
        )

    def gathers(source):
        return [block_copy(source, me, target) for target in far + [mate]]

    @pl.when(late == 0)
    def _():
        prepare()
        own_grad.wait()
        pl.semaphore_wait(barrier, n - 1)
        for copy in gathers(gathered.at[me]):
            copy.start()

    @pl.when(late == 1)
    def _():
        pl.semaphore_wait(barrier, n - 1)
        for copy in gathers(grad_hbm):
            copy.start()
        prepare()
        own_grad.wait()

    mixed = [jnp.zeros((y_count, CHANNELS), jnp.float32) for _ in range(x_rows)]
    hand_on = [block_copy(gathered.at[block], block, mate) for block in far]
    for slot in [me, mate] + far + handed:
        if slot is not me:
            block_copy(gathered.at[slot], slot, mate).wait_recv()
        for block, copy in zip(far, hand_on):
            if slot is block:
                copy.start()
        block = gathered[slot].astype(jnp.float32)
        rows = x_rows * y_count
        wide[pl.ds(pl.multiple_of(slot * rows, 8), rows), :] = block
        for r in range(x_rows):
            row = block[r * y_count : (r + 1) * y_count, :]
            factor = spread[pl.ds(slot * x_rows + r, 1), :]
            for x in range(x_rows):
                mixed[x] += row * factor[:, x * CHANNELS : (x + 1) * CHANNELS]
    grad_columns = jnp.concatenate(
        [
            wide[pl.ds(me * y_rows + y, x_count, stride=y_count), :]
            for y in range(y_rows)
        ],
        axis=1,
    )
    grad_columns = by_head(grad_columns)
    mixed = by_head(jnp.concatenate(mixed, axis=1).astype(jnp.bfloat16).astype(jnp.float32))
    query_x_term, key_x_term = factor_terms(
        kernel_x[...],
        kernel_x_turned[...],
        grad_columns,
        cached_lanes[...],
        query_x[...],
        key_x_ref[...],
    )
    query_y_term, key_y_term = factor_terms(
        kernel_y[...],
        kernel_y_turned[...],
        mixed,
        values_lanes[...],
        query_y[...],
        key_y_ref[...],
    )
    first = 0
    for term, count in (
        (query_x_term, x_rows),
        (key_x_term, x_rows),
        (query_y_term, y_rows),
        (key_y_term, y_rows),
    ):
        packing[pl.ds(n * first, n * count), :] = term
        for r in range(count):
            outgoing[:, first + r, :] = packing[
                pl.ds(n * first + r, n, stride=count), :
            ]
        first += count
    terms = []
    for peer in peers:
        copy = pltpu.make_async_remote_copy(
            src_ref=outgoing.at[peer],
            dst_ref=incoming.at[me],
            send_sem=term_send.at[peer],
            recv_sem=term_recv.at[me],
            device_id={"slab": peer},
            device_id_type=MESH,
        )
        copy.start()
        terms.append(copy)

    grad_values = jnp.dot(
        kernel_y_turned[...].astype(jnp.bfloat16), mixed, preferred_element_type=jnp.float32
    )
    for x in range(x_rows):
        grad_values_ref[x] = grad_values[:, x * CHANNELS : (x + 1) * CHANNELS].astype(
            grad_values_ref.dtype
        )

    for copy in gathers(gathered.at[me]) + hand_on + terms:
        copy.wait_send()
    total = outgoing[me]
    for peer in peers[::-1]:
        pltpu.make_async_remote_copy(
            src_ref=outgoing.at[peer],
            dst_ref=incoming.at[peer],
            send_sem=term_send.at[peer],
            recv_sem=term_recv.at[peer],
            device_id={"slab": peer},
            device_id_type=MESH,
        ).wait_recv()
        total += incoming[peer]
    factors_ref[...] = total * (1.0 / math.sqrt(HEAD))


def in_head(head, columns):
    lanes = lax.broadcasted_iota(jnp.int32, (1, CHANNELS), 1)
    mask = (lanes >= head * HEAD) & (lanes < (head + 1) * HEAD)
    return jnp.concatenate([mask] * (columns // CHANNELS), axis=1)


def by_head(array):
    return jnp.concatenate(
        [jnp.where(in_head(head, array.shape[1]), array, 0.0) for head in range(HEADS)], axis=0
    ).astype(jnp.bfloat16)


def per_head(array):
    rows = array.shape[0] // HEADS
    picked = array[:rows]
    for head in range(1, HEADS):
        picked = jnp.where(
            in_head(head, array.shape[1]), array[head * rows : (head + 1) * rows], picked
        )
    return picked


def rows_by_rows(left, right):
    return lax.dot_general(left, right, ROWS_BY_ROWS, preferred_element_type=jnp.float32)


def both_kernels(queries, key_rows):
    kernels = []
    for scores, axis in (
        (rows_by_rows(queries, key_rows), 1),
        (rows_by_rows(key_rows, queries), 0),
    ):
        scores = scores / math.sqrt(HEAD)
        weights = jnp.exp(scores - jnp.max(scores, axis=axis, keepdims=True))
        kernels.append(weights / jnp.sum(weights, axis=axis, keepdims=True))
    return kernels


def weighted_parts(kernel, coupling, axis):
    delta = jnp.sum(kernel * coupling, axis=axis, keepdims=True)
    weighted = kernel * (coupling - delta)
    high = weighted.astype(jnp.bfloat16)
    return high, (weighted - high.astype(jnp.float32)).astype(jnp.bfloat16)


def factor_terms(kernel, kernel_turned, left, right, queries, key_rows):
    high, low = weighted_parts(kernel, rows_by_rows(left, right), 1)
    query_term = jnp.dot(high, key_rows, preferred_element_type=jnp.float32) + jnp.dot(
        low, key_rows, preferred_element_type=jnp.float32
    )
    high, low = weighted_parts(kernel_turned, rows_by_rows(right, left), 0)
    key_term = jnp.dot(high, queries, preferred_element_type=jnp.float32) + jnp.dot(
        low, queries, preferred_element_type=jnp.float32
    )
    return per_head(query_term), key_term


def hand_out_kernel(values_ref, factors_ref, *out_refs):
    out_refs[0][...] = values_ref[...]
    start = 0
    for out_ref in out_refs[1:]:
        out_ref[...] = factors_ref[start : start + out_ref.shape[0], :]
        start += out_ref.shape[0]


def gathered_form(n, grad_out, cached, values, query_x, key_x, query_y, key_y):
    x_rows, y_count = grad_out.shape[:2]
    x_count, y_rows = cached.shape[:2]
    term_rows = 2 * (x_rows + y_rows)
    vmem = pl.BlockSpec(memory_space=pltpu.VMEM)
    grad_values, factors = pl.pallas_call(
        functools.partial(gather_kernel, n, x_rows, y_rows),
        out_shape=(
            pltpu.VMEM(values.shape, values.dtype),
            pltpu.VMEM((term_rows, CHANNELS), jnp.float32),
        ),
        in_specs=[pl.BlockSpec(memory_space=pltpu.HBM)] * 7,
        out_specs=(vmem, vmem),
        scratch_shapes=[
            pltpu.VMEM((n, x_rows * y_count, CHANNELS), jnp.bfloat16),
            pltpu.VMEM((y_rows * x_count, CHANNELS), jnp.bfloat16),
            pltpu.VMEM((x_rows * y_count, CHANNELS), jnp.bfloat16),
            pltpu.VMEM(query_x.shape, query_x.dtype),
            pltpu.VMEM(key_x.shape, key_x.dtype),
            pltpu.VMEM(query_y.shape, query_y.dtype),
            pltpu.VMEM(key_y.shape, key_y.dtype),
            pltpu.VMEM((HEADS * x_count, CHANNELS), jnp.bfloat16),
            pltpu.VMEM((HEADS * y_count, CHANNELS), jnp.bfloat16),
            pltpu.VMEM((HEADS * x_count, x_count), jnp.float32),
            pltpu.VMEM((x_count, HEADS * x_count), jnp.float32),
            pltpu.VMEM((HEADS * y_count, y_count), jnp.float32),
            pltpu.VMEM((y_count, HEADS * y_count), jnp.float32),
            pltpu.VMEM((x_count, y_rows * CHANNELS), jnp.bfloat16),
            pltpu.VMEM((y_count, x_rows * CHANNELS), jnp.bfloat16),
            pltpu.VMEM((x_count, x_rows * CHANNELS), jnp.float32),
            pltpu.VMEM(((x_count + 1) * y_count, CHANNELS), jnp.float32),
            pltpu.VMEM((2 * (x_count + y_count) + 8, CHANNELS), jnp.float32),
            pltpu.VMEM((n, term_rows, CHANNELS), jnp.float32),
            pltpu.VMEM((n, term_rows, CHANNELS), jnp.float32),
            pltpu.SemaphoreType.DMA((7,)),
            pltpu.SemaphoreType.DMA((n, n)),
            pltpu.SemaphoreType.DMA((n,)),
            pltpu.SemaphoreType.DMA((n,)),
            pltpu.SemaphoreType.DMA((n,)),
        ],
        compiler_params=pltpu.CompilerParams(
            collective_id=0, has_side_effects=True, vmem_limit_bytes=KERNEL_BYTES
        ),
    )(
        *(
            pltpu.with_memory_space_constraint(array, pltpu.HBM)
            for array in (
                grad_out.reshape(x_rows * y_count, CHANNELS),
                cached.transpose(1, 0, 2).reshape(y_rows * x_count, CHANNELS),
                values.reshape(x_rows * y_count, CHANNELS),
                query_x,
                key_x,
                query_y,
                key_y,
            )
        )
    )
    counts = (x_rows, x_rows, y_rows, y_rows)
    return pl.pallas_call(
        hand_out_kernel,
        out_shape=(jax.ShapeDtypeStruct(values.shape, values.dtype),)
        + tuple(jax.ShapeDtypeStruct((count, CHANNELS), jnp.float32) for count in counts),
        in_specs=[vmem] * 2,
        out_specs=(vmem,) * 5,
        compiler_params=pltpu.CompilerParams(vmem_limit_bytes=KERNEL_BYTES),
    )(grad_values, factors)


GATHERED_BYTES = 1 << 20
KERNEL_BYTES = 16 << 20


def on_device(n, *arrays):
    if n % 2 == 0 and arrays[0].size * arrays[0].dtype.itemsize * n <= GATHERED_BYTES:
        return gathered_form(n, *arrays)
    return exchanged_form(*arrays)


def solution(mesh):
    return jax.shard_map(
        functools.partial(on_device, mesh.shape["slab"]),
        mesh=mesh,
        in_specs=(
            P(("traj", "slab"), None, None),
            P("traj", "slab", None),
            P(("traj", "slab"), None, None),
            P("traj", None),
            P("traj", None),
            P("traj", None),
            P("traj", None),
        ),
        out_specs=(
            P(("traj", "slab"), None, None),
            P(("traj", "slab"), None),
            P(("traj", "slab"), None),
            P(("traj", "slab"), None),
            P(("traj", "slab"), None),
        ),
        check_vma=False,
    )
```

```python
import functools
import math

import jax
import jax.numpy as jnp
from jax import lax
from jax.experimental import pallas as pl
from jax.experimental.pallas import tpu as pltpu
from jax.sharding import PartitionSpec as P

HEADS = 4
HEAD = 32
CHANNELS = HEADS * HEAD


def axis_kernel(queries, key_rows):
    scores = jnp.dot(queries, key_rows.T, preferred_element_type=jnp.float32) / math.sqrt(HEAD)
    return jax.nn.softmax(scores, axis=1)


def local_terms(kernel, coupling, queries, key_rows):
    row_delta = jnp.sum(kernel * coupling, axis=1)
    weighted = kernel * coupling
    grad_query = jnp.dot(
        weighted, key_rows.astype(jnp.float32), precision=lax.Precision.HIGHEST
    ) / math.sqrt(HEAD)
    grad_key = jnp.dot(
        weighted.T, queries.astype(jnp.float32), precision=lax.Precision.HIGHEST
    ) / math.sqrt(HEAD)
    return (grad_query, grad_key, row_delta)


def corrections(own_rows, own_cols, delta_total, queries, key_rows, start, count):
    own_delta = lax.dynamic_slice_in_dim(delta_total, start, count, 0)
    query_fix = (
        own_delta[:, None]
        * jnp.dot(own_rows, key_rows.astype(jnp.float32), precision=lax.Precision.HIGHEST)
        / math.sqrt(HEAD)
    )
    key_fix = jnp.dot(
        own_cols.T,
        delta_total[:, None] * queries.astype(jnp.float32),
        precision=lax.Precision.HIGHEST,
    ) / math.sqrt(HEAD)
    return (query_fix, key_fix)


def exchanged_form(grad_out, cached, values, query_x, key_x, query_y, key_y):
    index = lax.axis_index("slab")
    x_rows = grad_out.shape[0]
    x_count = cached.shape[0]
    y_rows = cached.shape[1]
    x_start = index * x_rows
    y_start = index * y_rows
    grad_columns = lax.all_to_all(grad_out, "slab", split_axis=1, concat_axis=0, tiled=True)
    mixed_heads = []
    query_terms = []
    key_terms = []
    delta_terms = []
    row_slices = []
    col_slices = []
    for head_index in range(HEADS):
        offset = head_index * HEAD
        head_query = query_x[:, offset : offset + HEAD]
        head_key = key_x[:, offset : offset + HEAD]
        kernel = axis_kernel(head_query, head_key)
        grad_rows = grad_columns[:, :, offset : offset + HEAD].reshape(x_count, y_rows * HEAD)
        saved_rows = cached[:, :, offset : offset + HEAD].reshape(x_count, y_rows * HEAD)
        grad_mixed = lax.dot_general(
            kernel.astype(jnp.bfloat16),
            grad_rows,
            (((0,), (0,)), ((), ())),
            preferred_element_type=jnp.float32,
        ).astype(jnp.bfloat16)
        coupling = lax.dot_general(
            grad_rows, saved_rows, (((1,), (1,)), ((), ())), preferred_element_type=jnp.float32
        )
        grad_query, grad_key, row_delta = local_terms(kernel, coupling, head_query, head_key)
        query_terms.append(grad_query)
        key_terms.append(grad_key)
        delta_terms.append(row_delta)
        row_slices.append(lax.dynamic_slice_in_dim(kernel, x_start, x_rows, 0))
        col_slices.append(lax.dynamic_slice_in_dim(kernel, x_start, x_rows, 1))
        mixed_heads.append(grad_mixed.reshape(x_count, y_rows, HEAD))
    mixed_rows = lax.all_to_all(
        jnp.concatenate(mixed_heads, axis=2), "slab", split_axis=0, concat_axis=1, tiled=True
    )
    x_delta_total = lax.psum(jnp.stack(delta_terms), "slab")
    query_x_grad, key_x_grad = (
        lax.psum_scatter(
            jnp.concatenate(query_terms, axis=1), "slab", scatter_dimension=0, tiled=True
        ),
        lax.psum_scatter(
            jnp.concatenate(key_terms, axis=1), "slab", scatter_dimension=0, tiled=True
        ),
    )
    query_fixes = []
    key_fixes = []
    for head_index in range(HEADS):
        offset = head_index * HEAD
        query_fix, key_fix = corrections(
            row_slices[head_index],
            col_slices[head_index],
            x_delta_total[head_index],
            query_x[:, offset : offset + HEAD],
            key_x[:, offset : offset + HEAD],
            x_start,
            x_rows,
        )
        query_fixes.append(query_fix)
        key_fixes.append(key_fix)
    query_x_grad = query_x_grad - jnp.concatenate(query_fixes, axis=1)
    key_x_grad = key_x_grad - jnp.concatenate(key_fixes, axis=1)
    value_heads = []
    query_terms = []
    key_terms = []
    delta_terms = []
    row_slices = []
    col_slices = []
    for head_index in range(HEADS):
        offset = head_index * HEAD
        head_query = query_y[:, offset : offset + HEAD]
        head_key = key_y[:, offset : offset + HEAD]
        kernel = axis_kernel(head_query, head_key)
        mixed_head = mixed_rows[:, :, offset : offset + HEAD]
        value_head = values[:, :, offset : offset + HEAD]
        grad_value = jnp.einsum(
            "jk,xje->xke",
            kernel.astype(jnp.bfloat16),
            mixed_head,
            preferred_element_type=jnp.float32,
        )
        coupling = jnp.einsum(
            "xje,xke->jk", mixed_head, value_head, preferred_element_type=jnp.float32
        )
        grad_query, grad_key, row_delta = local_terms(kernel, coupling, head_query, head_key)
        query_terms.append(grad_query)
        key_terms.append(grad_key)
        delta_terms.append(row_delta)
        row_slices.append(lax.dynamic_slice_in_dim(kernel, y_start, y_rows, 0))
        col_slices.append(lax.dynamic_slice_in_dim(kernel, y_start, y_rows, 1))
        value_heads.append(grad_value.astype(jnp.bfloat16))
    y_delta_total = lax.psum(jnp.stack(delta_terms), "slab")
    query_y_grad, key_y_grad = (
        lax.psum_scatter(
            jnp.concatenate(query_terms, axis=1), "slab", scatter_dimension=0, tiled=True
        ),
        lax.psum_scatter(
            jnp.concatenate(key_terms, axis=1), "slab", scatter_dimension=0, tiled=True
        ),
    )
    query_fixes = []
    key_fixes = []
    for head_index in range(HEADS):
        offset = head_index * HEAD
        query_fix, key_fix = corrections(
            row_slices[head_index],
            col_slices[head_index],
            y_delta_total[head_index],
            query_y[:, offset : offset + HEAD],
            key_y[:, offset : offset + HEAD],
            y_start,
            y_rows,
        )
        query_fixes.append(query_fix)
        key_fixes.append(key_fix)
    query_y_grad = query_y_grad - jnp.concatenate(query_fixes, axis=1)
    key_y_grad = key_y_grad - jnp.concatenate(key_fixes, axis=1)
    grad_values = jnp.concatenate(value_heads, axis=2)
    return (grad_values, query_x_grad, key_x_grad, query_y_grad, key_y_grad)


MESH = pl.DeviceIdType.MESH
ROWS_BY_ROWS = (((1,), (1,)), ((), ()))


def gather_kernel(
    n,
    x_rows,
    y_rows,
    grad_hbm,
    cached_hbm,
    values_hbm,
    query_x_hbm,
    key_x_hbm,
    query_y_hbm,
    key_y_hbm,
    grad_values_ref,
    factors_ref,
    gathered,
    cached_ref,
    values_ref,
    query_x_ref,
    key_x_ref,
    query_y_ref,
    key_y_ref,
    query_x,
    query_y,
    kernel_x,
    kernel_x_turned,
    kernel_y,
    kernel_y_turned,
    cached_lanes,
    values_lanes,
    spread,
    wide,
    packing,
    outgoing,
    incoming,
    own_sems,
    gather_send,
    gather_recv,
    term_send,
    term_recv,
):
    me = lax.axis_index("slab")
    late = me // (n // 2)
    peers = [lax.rem(me + (2 * late - 1) * step + n, n) for step in range(1, n)]
    x_count, y_count = query_x_ref.shape[0], query_y_ref.shape[0]

    own_grad = pltpu.make_async_copy(grad_hbm, gathered.at[me], own_sems.at[6])
    own_grad.start()
    barrier = pltpu.get_barrier_semaphore()
    for peer in peers:
        pl.semaphore_signal(barrier, inc=1, device_id={"slab": peer}, device_id_type=MESH)
    own_pairs = (
        (query_x_hbm, query_x_ref),
        (key_x_hbm, key_x_ref),
        (query_y_hbm, query_y_ref),
        (key_y_hbm, key_y_ref),
        (cached_hbm, cached_ref),
        (values_hbm, values_ref),
    )
    own = [
        pltpu.make_async_copy(source, target, own_sems.at[place])
        for place, (source, target) in enumerate(own_pairs)
    ]
    for copy in own:
        copy.start()

    def prepare():
        for copy in own:
            copy.wait()
        for queries_ref, keys_ref, heads, kernel, turned in (
            (query_x_ref, key_x_ref, query_x, kernel_x, kernel_x_turned),
            (query_y_ref, key_y_ref, query_y, kernel_y, kernel_y_turned),
        ):
            heads[...] = by_head(queries_ref[...].astype(jnp.float32))
            kernel[...], turned[...] = both_kernels(heads[...], keys_ref[...])
        width = x_rows * CHANNELS
        rows = lax.broadcasted_iota(jnp.int32, (x_count, width), 0)
        lanes = lax.broadcasted_iota(jnp.int32, (x_count, width), 1)
        own_columns = (rows == me * x_rows + lanes // CHANNELS).astype(jnp.bfloat16)
        spread[...] = per_head(
            jnp.dot(
                kernel_x[...].astype(jnp.bfloat16),
                own_columns,
                preferred_element_type=jnp.float32,
            )
        )
        for source, count, target in (
            (cached_ref, x_count, cached_lanes),
            (values_ref, y_count, values_lanes),
        ):
            array = source[...].astype(jnp.float32)
            target[...] = jnp.concatenate(
                [array[r : r + count] for r in range(0, array.shape[0], count)], axis=1
            ).astype(jnp.bfloat16)

    def gathers(source):
        return [
            pltpu.make_async_remote_copy(
                src_ref=source,
                dst_ref=gathered.at[me],
                send_sem=gather_send.at[peer],
                recv_sem=gather_recv.at[me],
                device_id={"slab": peer},
                device_id_type=MESH,
            )
            for peer in peers
        ]

    @pl.when(late == 0)
    def _():
        prepare()
        own_grad.wait()
        pl.semaphore_wait(barrier, n - 1)
        for copy in gathers(gathered.at[me]):
            copy.start()

    @pl.when(late == 1)
    def _():
        pl.semaphore_wait(barrier, n - 1)
        for copy in gathers(grad_hbm):
            copy.start()
        prepare()
        own_grad.wait()

    mixed = [jnp.zeros((y_count, CHANNELS), jnp.float32) for _ in range(x_rows)]
    for slot in [me] + peers[::-1]:
        if slot is not me:
            pltpu.make_async_remote_copy(
                src_ref=gathered.at[me],
                dst_ref=gathered.at[slot],
                send_sem=gather_send.at[slot],
                recv_sem=gather_recv.at[slot],
                device_id={"slab": slot},
                device_id_type=MESH,
            ).wait_recv()
        block = gathered[slot].astype(jnp.float32)
        rows = x_rows * y_count
        wide[pl.ds(pl.multiple_of(slot * rows, 8), rows), :] = block
        for r in range(x_rows):
            row = block[r * y_count : (r + 1) * y_count, :]
            factor = spread[pl.ds(slot * x_rows + r, 1), :]
            for x in range(x_rows):
                mixed[x] += row * factor[:, x * CHANNELS : (x + 1) * CHANNELS]
    grad_columns = jnp.concatenate(
        [
            wide[pl.ds(me * y_rows + y, x_count, stride=y_count), :]
            for y in range(y_rows)
        ],
        axis=1,
    )
    grad_columns = by_head(grad_columns)
    mixed = by_head(jnp.concatenate(mixed, axis=1).astype(jnp.bfloat16).astype(jnp.float32))
    query_x_term, key_x_term = factor_terms(
        kernel_x[...],
        kernel_x_turned[...],
        grad_columns,
        cached_lanes[...],
        query_x[...],
        key_x_ref[...],
    )
    query_y_term, key_y_term = factor_terms(
        kernel_y[...],
        kernel_y_turned[...],
        mixed,
        values_lanes[...],
        query_y[...],
        key_y_ref[...],
    )
    first = 0
    for term, count in (
        (query_x_term, x_rows),
        (key_x_term, x_rows),
        (query_y_term, y_rows),
        (key_y_term, y_rows),
    ):
        packing[pl.ds(n * first, n * count), :] = term
        for r in range(count):
            outgoing[:, first + r, :] = packing[
                pl.ds(n * first + r, n, stride=count), :
            ]
        first += count
    terms = []
    for peer in peers:
        copy = pltpu.make_async_remote_copy(
            src_ref=outgoing.at[peer],
            dst_ref=incoming.at[me],
            send_sem=term_send.at[peer],
            recv_sem=term_recv.at[me],
            device_id={"slab": peer},
            device_id_type=MESH,
        )
        copy.start()
        terms.append(copy)

    grad_values = jnp.dot(
        kernel_y_turned[...].astype(jnp.bfloat16), mixed, preferred_element_type=jnp.float32
    )
    for x in range(x_rows):
        grad_values_ref[x] = grad_values[:, x * CHANNELS : (x + 1) * CHANNELS].astype(
            grad_values_ref.dtype
        )

    for copy in gathers(gathered.at[me]) + terms:
        copy.wait_send()
    total = outgoing[me]
    for peer in peers[::-1]:
        pltpu.make_async_remote_copy(
            src_ref=outgoing.at[peer],
            dst_ref=incoming.at[peer],
            send_sem=term_send.at[peer],
            recv_sem=term_recv.at[peer],
            device_id={"slab": peer},
            device_id_type=MESH,
        ).wait_recv()
        total += incoming[peer]
    factors_ref[...] = total * (1.0 / math.sqrt(HEAD))


def in_head(head, columns):
    lanes = lax.broadcasted_iota(jnp.int32, (1, CHANNELS), 1)
    mask = (lanes >= head * HEAD) & (lanes < (head + 1) * HEAD)
    return jnp.concatenate([mask] * (columns // CHANNELS), axis=1)


def by_head(array):
    return jnp.concatenate(
        [jnp.where(in_head(head, array.shape[1]), array, 0.0) for head in range(HEADS)], axis=0
    ).astype(jnp.bfloat16)


def per_head(array):
    rows = array.shape[0] // HEADS
    picked = array[:rows]
    for head in range(1, HEADS):
        picked = jnp.where(
            in_head(head, array.shape[1]), array[head * rows : (head + 1) * rows], picked
        )
    return picked


def rows_by_rows(left, right):
    return lax.dot_general(left, right, ROWS_BY_ROWS, preferred_element_type=jnp.float32)


def both_kernels(queries, key_rows):
    scores = rows_by_rows(key_rows, queries) / math.sqrt(HEAD)
    weights = jnp.exp(scores - jnp.max(scores, axis=0, keepdims=True))
    turned = weights / jnp.sum(weights, axis=0, keepdims=True)
    return turned.T, turned


def weighted_parts(kernel, coupling, axis):
    delta = jnp.sum(kernel * coupling, axis=axis, keepdims=True)
    weighted = kernel * (coupling - delta)
    high = weighted.astype(jnp.bfloat16)
    return high, (weighted - high.astype(jnp.float32)).astype(jnp.bfloat16)


def factor_terms(kernel, kernel_turned, left, right, queries, key_rows):
    high, low = weighted_parts(kernel, rows_by_rows(left, right), 1)
    query_term = jnp.dot(high, key_rows, preferred_element_type=jnp.float32) + jnp.dot(
        low, key_rows, preferred_element_type=jnp.float32
    )
    high, low = weighted_parts(kernel_turned, rows_by_rows(right, left), 0)
    key_term = jnp.dot(high, queries, preferred_element_type=jnp.float32) + jnp.dot(
        low, queries, preferred_element_type=jnp.float32
    )
    return per_head(query_term), key_term


def hand_out_kernel(values_ref, factors_ref, *out_refs):
    out_refs[0][...] = values_ref[...]
    start = 0
    for out_ref in out_refs[1:]:
        out_ref[...] = factors_ref[start : start + out_ref.shape[0], :]
        start += out_ref.shape[0]


def gathered_form(n, grad_out, cached, values, query_x, key_x, query_y, key_y):
    x_rows, y_count = grad_out.shape[:2]
    x_count, y_rows = cached.shape[:2]
    term_rows = 2 * (x_rows + y_rows)
    vmem = pl.BlockSpec(memory_space=pltpu.VMEM)
    grad_values, factors = pl.pallas_call(
        functools.partial(gather_kernel, n, x_rows, y_rows),
        out_shape=(
            pltpu.VMEM(values.shape, values.dtype),
            pltpu.VMEM((term_rows, CHANNELS), jnp.float32),
        ),
        in_specs=[pl.BlockSpec(memory_space=pltpu.HBM)] * 7,
        out_specs=(vmem, vmem),
        scratch_shapes=[
            pltpu.VMEM((n, x_rows * y_count, CHANNELS), jnp.bfloat16),
            pltpu.VMEM((y_rows * x_count, CHANNELS), jnp.bfloat16),
            pltpu.VMEM((x_rows * y_count, CHANNELS), jnp.bfloat16),
            pltpu.VMEM(query_x.shape, query_x.dtype),
            pltpu.VMEM(key_x.shape, key_x.dtype),
            pltpu.VMEM(query_y.shape, query_y.dtype),
            pltpu.VMEM(key_y.shape, key_y.dtype),
            pltpu.VMEM((HEADS * x_count, CHANNELS), jnp.bfloat16),
            pltpu.VMEM((HEADS * y_count, CHANNELS), jnp.bfloat16),
            pltpu.VMEM((HEADS * x_count, x_count), jnp.float32),
            pltpu.VMEM((x_count, HEADS * x_count), jnp.float32),
            pltpu.VMEM((HEADS * y_count, y_count), jnp.float32),
            pltpu.VMEM((y_count, HEADS * y_count), jnp.float32),
            pltpu.VMEM((x_count, y_rows * CHANNELS), jnp.bfloat16),
            pltpu.VMEM((y_count, x_rows * CHANNELS), jnp.bfloat16),
            pltpu.VMEM((x_count, x_rows * CHANNELS), jnp.float32),
            pltpu.VMEM(((x_count + 1) * y_count, CHANNELS), jnp.float32),
            pltpu.VMEM((2 * (x_count + y_count) + 8, CHANNELS), jnp.float32),
            pltpu.VMEM((n, term_rows, CHANNELS), jnp.float32),
            pltpu.VMEM((n, term_rows, CHANNELS), jnp.float32),
            pltpu.SemaphoreType.DMA((7,)),
            pltpu.SemaphoreType.DMA((n,)),
            pltpu.SemaphoreType.DMA((n,)),
            pltpu.SemaphoreType.DMA((n,)),
            pltpu.SemaphoreType.DMA((n,)),
        ],
        compiler_params=pltpu.CompilerParams(
            collective_id=0, has_side_effects=True, vmem_limit_bytes=KERNEL_BYTES
        ),
    )(
        *(
            pltpu.with_memory_space_constraint(array, pltpu.HBM)
            for array in (
                grad_out.reshape(x_rows * y_count, CHANNELS),
                cached.transpose(1, 0, 2).reshape(y_rows * x_count, CHANNELS),
                values.reshape(x_rows * y_count, CHANNELS),
                query_x,
                key_x,
                query_y,
                key_y,
            )
        )
    )
    counts = (x_rows, x_rows, y_rows, y_rows)
    return pl.pallas_call(
        hand_out_kernel,
        out_shape=(jax.ShapeDtypeStruct(values.shape, values.dtype),)
        + tuple(jax.ShapeDtypeStruct((count, CHANNELS), jnp.float32) for count in counts),
        in_specs=[vmem] * 2,
        out_specs=(vmem,) * 5,
        compiler_params=pltpu.CompilerParams(vmem_limit_bytes=KERNEL_BYTES),
    )(grad_values, factors)


GATHERED_BYTES = 1 << 20
KERNEL_BYTES = 16 << 20


def on_device(n, *arrays):
    if n % 2 == 0 and arrays[0].size * arrays[0].dtype.itemsize * n <= GATHERED_BYTES:
        return gathered_form(n, *arrays)
    return exchanged_form(*arrays)


def solution(mesh):
    return jax.shard_map(
        functools.partial(on_device, mesh.shape["slab"]),
        mesh=mesh,
        in_specs=(
            P(("traj", "slab"), None, None),
            P("traj", "slab", None),
            P(("traj", "slab"), None, None),
            P("traj", None),
            P("traj", None),
            P("traj", None),
            P("traj", None),
        ),
        out_specs=(
            P(("traj", "slab"), None, None),
            P(("traj", "slab"), None),
            P(("traj", "slab"), None),
            P(("traj", "slab"), None),
            P(("traj", "slab"), None),
        ),
        check_vma=False,
    )
```

```python
import functools
import math

import jax
import jax.numpy as jnp
from jax import lax
from jax.experimental import pallas as pl
from jax.experimental.pallas import tpu as pltpu
from jax.sharding import PartitionSpec as P

HEADS = 4
HEAD = 32
CHANNELS = HEADS * HEAD


def axis_kernel(queries, key_rows):
    scores = jnp.dot(queries, key_rows.T, preferred_element_type=jnp.float32) / math.sqrt(HEAD)
    return jax.nn.softmax(scores, axis=1)


def local_terms(kernel, coupling, queries, key_rows):
    row_delta = jnp.sum(kernel * coupling, axis=1)
    weighted = kernel * coupling
    grad_query = jnp.dot(
        weighted, key_rows.astype(jnp.float32), precision=lax.Precision.HIGHEST
    ) / math.sqrt(HEAD)
    grad_key = jnp.dot(
        weighted.T, queries.astype(jnp.float32), precision=lax.Precision.HIGHEST
    ) / math.sqrt(HEAD)
    return (grad_query, grad_key, row_delta)


def corrections(own_rows, own_cols, delta_total, queries, key_rows, start, count):
    own_delta = lax.dynamic_slice_in_dim(delta_total, start, count, 0)
    query_fix = (
        own_delta[:, None]
        * jnp.dot(own_rows, key_rows.astype(jnp.float32), precision=lax.Precision.HIGHEST)
        / math.sqrt(HEAD)
    )
    key_fix = jnp.dot(
        own_cols.T,
        delta_total[:, None] * queries.astype(jnp.float32),
        precision=lax.Precision.HIGHEST,
    ) / math.sqrt(HEAD)
    return (query_fix, key_fix)


def exchanged_form(grad_out, cached, values, query_x, key_x, query_y, key_y):
    index = lax.axis_index("slab")
    x_rows = grad_out.shape[0]
    x_count = cached.shape[0]
    y_rows = cached.shape[1]
    x_start = index * x_rows
    y_start = index * y_rows
    grad_columns = lax.all_to_all(grad_out, "slab", split_axis=1, concat_axis=0, tiled=True)
    mixed_heads = []
    query_terms = []
    key_terms = []
    delta_terms = []
    row_slices = []
    col_slices = []
    for head_index in range(HEADS):
        offset = head_index * HEAD
        head_query = query_x[:, offset : offset + HEAD]
        head_key = key_x[:, offset : offset + HEAD]
        kernel = axis_kernel(head_query, head_key)
        grad_rows = grad_columns[:, :, offset : offset + HEAD].reshape(x_count, y_rows * HEAD)
        saved_rows = cached[:, :, offset : offset + HEAD].reshape(x_count, y_rows * HEAD)
        grad_mixed = lax.dot_general(
            kernel.astype(jnp.bfloat16),
            grad_rows,
            (((0,), (0,)), ((), ())),
            preferred_element_type=jnp.float32,
        ).astype(jnp.bfloat16)
        coupling = lax.dot_general(
            grad_rows, saved_rows, (((1,), (1,)), ((), ())), preferred_element_type=jnp.float32
        )
        grad_query, grad_key, row_delta = local_terms(kernel, coupling, head_query, head_key)
        query_terms.append(grad_query)
        key_terms.append(grad_key)
        delta_terms.append(row_delta)
        row_slices.append(lax.dynamic_slice_in_dim(kernel, x_start, x_rows, 0))
        col_slices.append(lax.dynamic_slice_in_dim(kernel, x_start, x_rows, 1))
        mixed_heads.append(grad_mixed.reshape(x_count, y_rows, HEAD))
    mixed_rows = lax.all_to_all(
        jnp.concatenate(mixed_heads, axis=2), "slab", split_axis=0, concat_axis=1, tiled=True
    )
    x_delta_total = lax.psum(jnp.stack(delta_terms), "slab")
    query_x_grad, key_x_grad = (
        lax.psum_scatter(
            jnp.concatenate(query_terms, axis=1), "slab", scatter_dimension=0, tiled=True
        ),
        lax.psum_scatter(
            jnp.concatenate(key_terms, axis=1), "slab", scatter_dimension=0, tiled=True
        ),
    )
    query_fixes = []
    key_fixes = []
    for head_index in range(HEADS):
        offset = head_index * HEAD
        query_fix, key_fix = corrections(
            row_slices[head_index],
            col_slices[head_index],
            x_delta_total[head_index],
            query_x[:, offset : offset + HEAD],
            key_x[:, offset : offset + HEAD],
            x_start,
            x_rows,
        )
        query_fixes.append(query_fix)
        key_fixes.append(key_fix)
    query_x_grad = query_x_grad - jnp.concatenate(query_fixes, axis=1)
    key_x_grad = key_x_grad - jnp.concatenate(key_fixes, axis=1)
    value_heads = []
    query_terms = []
    key_terms = []
    delta_terms = []
    row_slices = []
    col_slices = []
    for head_index in range(HEADS):
        offset = head_index * HEAD
        head_query = query_y[:, offset : offset + HEAD]
        head_key = key_y[:, offset : offset + HEAD]
        kernel = axis_kernel(head_query, head_key)
        mixed_head = mixed_rows[:, :, offset : offset + HEAD]
        value_head = values[:, :, offset : offset + HEAD]
        grad_value = jnp.einsum(
            "jk,xje->xke",
            kernel.astype(jnp.bfloat16),
            mixed_head,
            preferred_element_type=jnp.float32,
        )
        coupling = jnp.einsum(
            "xje,xke->jk", mixed_head, value_head, preferred_element_type=jnp.float32
        )
        grad_query, grad_key, row_delta = local_terms(kernel, coupling, head_query, head_key)
        query_terms.append(grad_query)
        key_terms.append(grad_key)
        delta_terms.append(row_delta)
        row_slices.append(lax.dynamic_slice_in_dim(kernel, y_start, y_rows, 0))
        col_slices.append(lax.dynamic_slice_in_dim(kernel, y_start, y_rows, 1))
        value_heads.append(grad_value.astype(jnp.bfloat16))
    y_delta_total = lax.psum(jnp.stack(delta_terms), "slab")
    query_y_grad, key_y_grad = (
        lax.psum_scatter(
            jnp.concatenate(query_terms, axis=1), "slab", scatter_dimension=0, tiled=True
        ),
        lax.psum_scatter(
            jnp.concatenate(key_terms, axis=1), "slab", scatter_dimension=0, tiled=True
        ),
    )
    query_fixes = []
    key_fixes = []
    for head_index in range(HEADS):
        offset = head_index * HEAD
        query_fix, key_fix = corrections(
            row_slices[head_index],
            col_slices[head_index],
            y_delta_total[head_index],
            query_y[:, offset : offset + HEAD],
            key_y[:, offset : offset + HEAD],
            y_start,
            y_rows,
        )
        query_fixes.append(query_fix)
        key_fixes.append(key_fix)
    query_y_grad = query_y_grad - jnp.concatenate(query_fixes, axis=1)
    key_y_grad = key_y_grad - jnp.concatenate(key_fixes, axis=1)
    grad_values = jnp.concatenate(value_heads, axis=2)
    return (grad_values, query_x_grad, key_x_grad, query_y_grad, key_y_grad)


MESH = pl.DeviceIdType.MESH
ROWS_BY_ROWS = (((1,), (1,)), ((), ()))


def gather_kernel(
    n,
    x_rows,
    y_rows,
    grad_hbm,
    cached_hbm,
    values_hbm,
    query_x_hbm,
    key_x_hbm,
    query_y_hbm,
    key_y_hbm,
    grad_values_ref,
    factors_ref,
    gathered,
    cached_ref,
    values_ref,
    query_x_ref,
    key_x_ref,
    query_y_ref,
    key_y_ref,
    query_x,
    query_y,
    kernel_x,
    kernel_x_turned,
    kernel_y,
    kernel_y_turned,
    cached_lanes,
    values_lanes,
    spread,
    wide,
    packing,
    outgoing,
    incoming,
    own_sems,
    gather_send,
    gather_recv,
    term_send,
    term_recv,
):
    me = lax.axis_index("slab")
    late = me // (n // 2)
    peers = [lax.rem(me + (2 * late - 1) * step + n, n) for step in range(1, n)]
    x_count, y_count = query_x_ref.shape[0], query_y_ref.shape[0]

    own_grad = pltpu.make_async_copy(grad_hbm, gathered.at[me], own_sems.at[6])
    own_grad.start()
    barrier = pltpu.get_barrier_semaphore()
    for peer in peers:
        pl.semaphore_signal(barrier, inc=1, device_id={"slab": peer}, device_id_type=MESH)
    own_pairs = (
        (query_x_hbm, query_x_ref),
        (key_x_hbm, key_x_ref),
        (query_y_hbm, query_y_ref),
        (key_y_hbm, key_y_ref),
        (cached_hbm, cached_ref),
        (values_hbm, values_ref),
    )
    own = [
        pltpu.make_async_copy(source, target, own_sems.at[place])
        for place, (source, target) in enumerate(own_pairs)
    ]
    for copy in own:
        copy.start()

    def prepare():
        for copy in own:
            copy.wait()
        for queries_ref, keys_ref, heads, kernel, turned in (
            (query_x_ref, key_x_ref, query_x, kernel_x, kernel_x_turned),
            (query_y_ref, key_y_ref, query_y, kernel_y, kernel_y_turned),
        ):
            heads[...] = by_head(queries_ref[...].astype(jnp.float32))
            kernel[...], turned[...] = both_kernels(heads[...], keys_ref[...])
        width = x_rows * CHANNELS
        rows = lax.broadcasted_iota(jnp.int32, (x_count, width), 0)
        lanes = lax.broadcasted_iota(jnp.int32, (x_count, width), 1)
        own_columns = (rows == me * x_rows + lanes // CHANNELS).astype(jnp.bfloat16)
        spread[...] = per_head(
            jnp.dot(
                kernel_x[...].astype(jnp.bfloat16),
                own_columns,
                preferred_element_type=jnp.float32,
            )
        )
        for source, count, target in (
            (cached_ref, x_count, cached_lanes),
            (values_ref, y_count, values_lanes),
        ):
            array = source[...].astype(jnp.float32)
            target[...] = jnp.concatenate(
                [array[r : r + count] for r in range(0, array.shape[0], count)], axis=1
            ).astype(jnp.bfloat16)

    def gathers():
        return [
            pltpu.make_async_remote_copy(
                src_ref=gathered.at[me],
                dst_ref=gathered.at[me],
                send_sem=gather_send.at[peer],
                recv_sem=gather_recv.at[me],
                device_id={"slab": peer},
                device_id_type=MESH,
            )
            for peer in peers
        ]

    @pl.when(late == 0)
    def _():
        prepare()
        own_grad.wait()
        pl.semaphore_wait(barrier, n - 1)
        for copy in gathers():
            copy.start()

    @pl.when(late == 1)
    def _():
        own_grad.wait()
        pl.semaphore_wait(barrier, n - 1)
        for copy in gathers():
            copy.start()
        prepare()

    mixed = [jnp.zeros((y_count, CHANNELS), jnp.float32) for _ in range(x_rows)]
    for slot in [me] + peers[::-1]:
        if slot is not me:
            pltpu.make_async_remote_copy(
                src_ref=gathered.at[me],
                dst_ref=gathered.at[slot],
                send_sem=gather_send.at[slot],
                recv_sem=gather_recv.at[slot],
                device_id={"slab": slot},
                device_id_type=MESH,
            ).wait_recv()
        block = gathered[slot].astype(jnp.float32)
        rows = x_rows * y_count
        wide[pl.ds(pl.multiple_of(slot * rows, 8), rows), :] = block
        for r in range(x_rows):
            row = block[r * y_count : (r + 1) * y_count, :]
            factor = spread[pl.ds(slot * x_rows + r, 1), :]
            for x in range(x_rows):
                mixed[x] += row * factor[:, x * CHANNELS : (x + 1) * CHANNELS]
    grad_columns = jnp.concatenate(
        [
            wide[pl.ds(me * y_rows + y, x_count, stride=y_count), :]
            for y in range(y_rows)
        ],
        axis=1,
    )
    grad_columns = by_head(grad_columns)
    mixed = by_head(jnp.concatenate(mixed, axis=1).astype(jnp.bfloat16).astype(jnp.float32))
    query_x_term, key_x_term = factor_terms(
        kernel_x[...],
        kernel_x_turned[...],
        grad_columns,
        cached_lanes[...],
        query_x[...],
        key_x_ref[...],
    )
    query_y_term, key_y_term = factor_terms(
        kernel_y[...],
        kernel_y_turned[...],
        mixed,
        values_lanes[...],
        query_y[...],
        key_y_ref[...],
    )
    first = 0
    for term, count in (
        (query_x_term, x_rows),
        (key_x_term, x_rows),
        (query_y_term, y_rows),
        (key_y_term, y_rows),
    ):
        packing[pl.ds(n * first, n * count), :] = term
        for r in range(count):
            outgoing[:, first + r, :] = packing[
                pl.ds(n * first + r, n, stride=count), :
            ]
        first += count
    terms = []
    for peer in peers:
        copy = pltpu.make_async_remote_copy(
            src_ref=outgoing.at[peer],
            dst_ref=incoming.at[me],
            send_sem=term_send.at[peer],
            recv_sem=term_recv.at[me],
            device_id={"slab": peer},
            device_id_type=MESH,
        )
        copy.start()
        terms.append(copy)

    grad_values = jnp.dot(
        kernel_y_turned[...].astype(jnp.bfloat16), mixed, preferred_element_type=jnp.float32
    )
    for x in range(x_rows):
        grad_values_ref[x] = grad_values[:, x * CHANNELS : (x + 1) * CHANNELS].astype(
            grad_values_ref.dtype
        )

    for copy in gathers() + terms:
        copy.wait_send()
    total = outgoing[me]
    for peer in peers[::-1]:
        pltpu.make_async_remote_copy(
            src_ref=outgoing.at[peer],
            dst_ref=incoming.at[peer],
            send_sem=term_send.at[peer],
            recv_sem=term_recv.at[peer],
            device_id={"slab": peer},
            device_id_type=MESH,
        ).wait_recv()
        total += incoming[peer]
    factors_ref[...] = total * (1.0 / math.sqrt(HEAD))


def in_head(head, columns):
    lanes = lax.broadcasted_iota(jnp.int32, (1, CHANNELS), 1)
    mask = (lanes >= head * HEAD) & (lanes < (head + 1) * HEAD)
    return jnp.concatenate([mask] * (columns // CHANNELS), axis=1)


def by_head(array):
    return jnp.concatenate(
        [jnp.where(in_head(head, array.shape[1]), array, 0.0) for head in range(HEADS)], axis=0
    ).astype(jnp.bfloat16)


def per_head(array):
    rows = array.shape[0] // HEADS
    picked = array[:rows]
    for head in range(1, HEADS):
        picked = jnp.where(
            in_head(head, array.shape[1]), array[head * rows : (head + 1) * rows], picked
        )
    return picked


def rows_by_rows(left, right):
    return lax.dot_general(left, right, ROWS_BY_ROWS, preferred_element_type=jnp.float32)


def both_kernels(queries, key_rows):
    scores = rows_by_rows(key_rows, queries) / math.sqrt(HEAD)
    weights = jnp.exp(scores - jnp.max(scores, axis=0, keepdims=True))
    turned = weights / jnp.sum(weights, axis=0, keepdims=True)
    return turned.T, turned


def weighted_parts(kernel, coupling, axis):
    delta = jnp.sum(kernel * coupling, axis=axis, keepdims=True)
    weighted = kernel * (coupling - delta)
    high = weighted.astype(jnp.bfloat16)
    return high, (weighted - high.astype(jnp.float32)).astype(jnp.bfloat16)


def factor_terms(kernel, kernel_turned, left, right, queries, key_rows):
    high, low = weighted_parts(kernel, rows_by_rows(left, right), 1)
    query_term = jnp.dot(high, key_rows, preferred_element_type=jnp.float32) + jnp.dot(
        low, key_rows, preferred_element_type=jnp.float32
    )
    high, low = weighted_parts(kernel_turned, rows_by_rows(right, left), 0)
    key_term = jnp.dot(high, queries, preferred_element_type=jnp.float32) + jnp.dot(
        low, queries, preferred_element_type=jnp.float32
    )
    return per_head(query_term), key_term


def hand_out_kernel(values_ref, factors_ref, *out_refs):
    out_refs[0][...] = values_ref[...]
    start = 0
    for out_ref in out_refs[1:]:
        out_ref[...] = factors_ref[start : start + out_ref.shape[0], :]
        start += out_ref.shape[0]


def gathered_form(n, grad_out, cached, values, query_x, key_x, query_y, key_y):
    x_rows, y_count = grad_out.shape[:2]
    x_count, y_rows = cached.shape[:2]
    term_rows = 2 * (x_rows + y_rows)
    vmem = pl.BlockSpec(memory_space=pltpu.VMEM)
    grad_values, factors = pl.pallas_call(
        functools.partial(gather_kernel, n, x_rows, y_rows),
        out_shape=(
            pltpu.VMEM(values.shape, values.dtype),
            pltpu.VMEM((term_rows, CHANNELS), jnp.float32),
        ),
        in_specs=[pl.BlockSpec(memory_space=pltpu.HBM)] * 7,
        out_specs=(vmem, vmem),
        scratch_shapes=[
            pltpu.VMEM((n, x_rows * y_count, CHANNELS), jnp.bfloat16),
            pltpu.VMEM((y_rows * x_count, CHANNELS), jnp.bfloat16),
            pltpu.VMEM((x_rows * y_count, CHANNELS), jnp.bfloat16),
            pltpu.VMEM(query_x.shape, query_x.dtype),
            pltpu.VMEM(key_x.shape, key_x.dtype),
            pltpu.VMEM(query_y.shape, query_y.dtype),
            pltpu.VMEM(key_y.shape, key_y.dtype),
            pltpu.VMEM((HEADS * x_count, CHANNELS), jnp.bfloat16),
            pltpu.VMEM((HEADS * y_count, CHANNELS), jnp.bfloat16),
            pltpu.VMEM((HEADS * x_count, x_count), jnp.float32),
            pltpu.VMEM((x_count, HEADS * x_count), jnp.float32),
            pltpu.VMEM((HEADS * y_count, y_count), jnp.float32),
            pltpu.VMEM((y_count, HEADS * y_count), jnp.float32),
            pltpu.VMEM((x_count, y_rows * CHANNELS), jnp.bfloat16),
            pltpu.VMEM((y_count, x_rows * CHANNELS), jnp.bfloat16),
            pltpu.VMEM((x_count, x_rows * CHANNELS), jnp.float32),
            pltpu.VMEM(((x_count + 1) * y_count, CHANNELS), jnp.float32),
            pltpu.VMEM((2 * (x_count + y_count) + 8, CHANNELS), jnp.float32),
            pltpu.VMEM((n, term_rows, CHANNELS), jnp.float32),
            pltpu.VMEM((n, term_rows, CHANNELS), jnp.float32),
            pltpu.SemaphoreType.DMA((7,)),
            pltpu.SemaphoreType.DMA((n,)),
            pltpu.SemaphoreType.DMA((n,)),
            pltpu.SemaphoreType.DMA((n,)),
            pltpu.SemaphoreType.DMA((n,)),
        ],
        compiler_params=pltpu.CompilerParams(
            collective_id=0, has_side_effects=True, vmem_limit_bytes=KERNEL_BYTES
        ),
    )(
        *(
            pltpu.with_memory_space_constraint(array, pltpu.HBM)
            for array in (
                grad_out.reshape(x_rows * y_count, CHANNELS),
                cached.transpose(1, 0, 2).reshape(y_rows * x_count, CHANNELS),
                values.reshape(x_rows * y_count, CHANNELS),
                query_x,
                key_x,
                query_y,
                key_y,
            )
        )
    )
    counts = (x_rows, x_rows, y_rows, y_rows)
    return pl.pallas_call(
        hand_out_kernel,
        out_shape=(jax.ShapeDtypeStruct(values.shape, values.dtype),)
        + tuple(jax.ShapeDtypeStruct((count, CHANNELS), jnp.float32) for count in counts),
        in_specs=[vmem] * 2,
        out_specs=(vmem,) * 5,
        compiler_params=pltpu.CompilerParams(vmem_limit_bytes=KERNEL_BYTES),
    )(grad_values, factors)


GATHERED_BYTES = 1 << 20
KERNEL_BYTES = 16 << 20


def on_device(n, *arrays):
    if n % 2 == 0 and arrays[0].size * arrays[0].dtype.itemsize * n <= GATHERED_BYTES:
        return gathered_form(n, *arrays)
    return exchanged_form(*arrays)


def solution(mesh):
    return jax.shard_map(
        functools.partial(on_device, mesh.shape["slab"]),
        mesh=mesh,
        in_specs=(
            P(("traj", "slab"), None, None),
            P("traj", "slab", None),
            P(("traj", "slab"), None, None),
            P("traj", None),
            P("traj", None),
            P("traj", None),
            P("traj", None),
        ),
        out_specs=(
            P(("traj", "slab"), None, None),
            P(("traj", "slab"), None),
            P(("traj", "slab"), None),
            P(("traj", "slab"), None),
            P(("traj", "slab"), None),
        ),
        check_vma=False,
    )
```
